128 devices in a mesh: res: 32 (over x, y_lo, z), seq: 4 (over y_hi, core).
Axes of the slice: x: 4, y: 4 (y_hi: 2, y_lo: 2; y = y_hi * 2 + y_lo), z: 4, core: 2. Of those that a mesh axis runs over, the one named last changes fastest.
Arguments:
- aligned_family_array: float32 [128, 768, 256], P('seq', 'res'), may hold values from -6 to 6
- couple_representation: float32 [768, 768, 128], P('res', 'seq'), may hold values from -6 to 6
- amino_real_flags: int32 [768], replicated, may hold values 0 or 1
- polymer_identity: int32 [768], replicated, may hold values from 0 to 3, as said below
- homolog_live_flags: int32 [128], replicated, may hold values 0 or 1
- projection_quartet_matrix: bfloat16 [256, 1024], replicated, may hold values from -0.8 to 0.8
- couple_shift_matrix: float32 [128, 8], replicated, may hold values from -0.5 to 0.5
- cross_polymer_score_shift: float32 [8], replicated, may hold values from -2 to 2
- mixing_exit_matrix: bfloat16 [256, 256], replicated, may hold values from -0.375 to 0.375
- factor_pair_matrices: bfloat16 [256, 64], replicated, may hold values from -0.375 to 0.375
- tensor_mean_matrix: float32 [1024, 128], replicated, may hold values from -1 to 1
Outputs:
- family_array_reweighted: float32 [128, 768, 256], P('seq', 'res')
- contact_grid_result: float32 [768, 768, 128], P('res', 'seq')
The draws below stay inside these ranges and needn't reach their ends.
Inputs may be any that keep to these rules, and one draw needn't show every extreme that they name: `polymer_identity`: each chain is one run of consecutive residues; there are at most four chains.
All inputs are finite; a program needn't handle non-finite values.
Results may differ from the reference program's by a relative error of at most 0.0029.
Values may be sent and summed in bfloat16 or wider, within the bound.
A program may use at most 320 MiB of HBM per device.

```python
import math
import jax
import jax.numpy as jnp
from jax import lax

CM = 256
CZ = 128
ATTENTION_HEADS = 8
HEAD_CHANNELS = 32
OPM = 32
RES_DEV = 24
RESIDUE_COUNT = 768
ROWS = 128
N_RES = 32


def draw_polymer_identity(key, part):
    key = jax.random.fold_in(key, 5)
    cuts = jax.random.randint(key, (3,), 1, RESIDUE_COUNT)
    position = jnp.arange(RESIDUE_COUNT)
    return jnp.sum(position[:, None] >= cuts[None, :], axis=1).astype(jnp.int32)


def draw_aligned_family_array(key, part):
    key = jax.random.fold_in(key, 11)
    k_base = jax.random.fold_in(key, 0)
    return jnp.clip(jax.random.normal(k_base, (ROWS, RESIDUE_COUNT, CM), jnp.float32), -6.0, 6.0)


def draw_projection_quartet_matrix(key, part):
    key = jax.random.fold_in(key, 13)
    k_base = jax.random.fold_in(key, 0)
    feature_width = ATTENTION_HEADS * HEAD_CHANNELS
    bound = min(6.0 / math.sqrt(CM), 0.78)
    value_rows = jax.random.normal(k_base, (CM, 4 * feature_width), jnp.float32) / math.sqrt(CM)
    return jnp.clip(value_rows, -bound, bound).astype(jnp.bfloat16)


def touch_ends(array, rng, least, high):
    place = [jax.random.randint(jax.random.fold_in(rng, axis), (), 0, length) for axis, length in enumerate(array.shape)]
    main_axis = array.shape.index(max(array.shape))
    neighbour = place[:main_axis] + [(place[main_axis] + 1) % array.shape[main_axis]] + place[main_axis + 1:]
    return array.at[tuple(place)].set(least).at[tuple(neighbour)].set(high)


def block_scale(stream_key, extent, cuts, least, largest):
    level, own = 1.0, jax.random.fold_in(stream_key, 6)
    for axis_at, shards_of in cuts:
        draws = jnp.exp(jax.random.uniform(jax.random.fold_in(own, axis_at), (shards_of,), jnp.float32, least / len(cuts), largest / len(cuts)))
        level = level * jnp.repeat(draws, extent[axis_at] // shards_of).reshape([-1 if axis == axis_at else 1 for axis in range(len(extent))])
    return level


def centred(stream_key, shape, deviation, most, cuts=(), held_as=jnp.bfloat16):
    drawn = jax.random.normal(stream_key, shape, jnp.float32) * deviation
    if len(cuts) > 0:
        drawn = block_scale(stream_key, shape, cuts, -0.22, 0.18) * drawn
    return jnp.clip(drawn, min=-most, max=most).astype(held_as)


def setup_inputs(seed: int = 0) -> dict:
    streams_of = jax.random.split(jax.random.key(seed), 12)
    return {
        "aligned_family_array": draw_aligned_family_array(jax.random.fold_in(streams_of[11], 71), 0),
        "couple_representation": centred(streams_of[1], (RESIDUE_COUNT, RESIDUE_COUNT, CZ), 1.0, 6.0, ((0, 32), (1, 4)), jnp.float32),
        "amino_real_flags": touch_ends((jax.random.randint(streams_of[2], (RESIDUE_COUNT,), 0, 8) < 7).astype(jnp.int32), jax.random.fold_in(streams_of[2], 1), 0, 1),
        "polymer_identity": draw_polymer_identity(jax.random.fold_in(streams_of[11], 71), 0),
        "homolog_live_flags": touch_ends((jax.random.randint(streams_of[4], (ROWS,), 0, 4) < 3).astype(jnp.int32), jax.random.fold_in(streams_of[4], 1), 0, 1),
        "projection_quartet_matrix": draw_projection_quartet_matrix(jax.random.fold_in(streams_of[11], 71), 0),
        "couple_shift_matrix": centred(streams_of[6], (CZ, ATTENTION_HEADS), CZ ** -0.5, 0.5, (), jnp.float32),
        "cross_polymer_score_shift": jnp.clip(jax.random.uniform(streams_of[7], (ATTENTION_HEADS,), jnp.float32, -2.0, 2.0), -2.0, 2.0),
        "mixing_exit_matrix": centred(streams_of[8], (ATTENTION_HEADS * HEAD_CHANNELS, CM), (ATTENTION_HEADS * HEAD_CHANNELS) ** -0.5, 0.375),
        "factor_pair_matrices": centred(streams_of[9], (CM, 2 * OPM), CM ** -0.5, 0.375),
        "tensor_mean_matrix": centred(streams_of[10], (OPM * OPM, CZ), OPM ** -0.5, 1.0, (), jnp.float32),
    }


def zscore_elements(value_rows):
    centre = lax.optimization_barrier(jnp.mean(value_rows, axis=-1, keepdims=True))
    spread = lax.optimization_barrier(jnp.mean((value_rows - centre) ** 2, axis=-1, keepdims=True))
    return (value_rows - centre) * lax.rsqrt(spread + 1e-05)

def reference(aligned_family_array, couple_representation, amino_real_flags, polymer_identity, homolog_live_flags, projection_quartet_matrix, couple_shift_matrix, cross_polymer_score_shift, mixing_exit_matrix, factor_pair_matrices, tensor_mean_matrix):
    feature_width = ATTENTION_HEADS * HEAD_CHANNELS
    standardized_stack = zscore_elements(aligned_family_array).astype(jnp.bfloat16)
    projected = jnp.dot(standardized_stack.reshape(-1, CM), projection_quartet_matrix, preferred_element_type=jnp.float32)
    projected = projected.astype(jnp.bfloat16).reshape(ROWS, RESIDUE_COUNT, 4 * feature_width)
    bias = jnp.einsum('ijc,ch->hij', zscore_elements(couple_representation), couple_shift_matrix, precision=lax.Precision.HIGHEST)
    differ = (polymer_identity[:, None] != polymer_identity[None, :]).astype(jnp.float32)
    bias = bias + cross_polymer_score_shift[:, None, None] * differ[None]
    key_live = amino_real_flags > 0

    def single_row(alignment_row):
        query_rows = alignment_row[:, :feature_width].astype(jnp.float32).reshape(RESIDUE_COUNT, ATTENTION_HEADS, HEAD_CHANNELS)
        key_rows = alignment_row[:, feature_width:2 * feature_width].astype(jnp.float32).reshape(RESIDUE_COUNT, ATTENTION_HEADS, HEAD_CHANNELS)
        value_rows = alignment_row[:, 2 * feature_width:3 * feature_width].astype(jnp.float32).reshape(RESIDUE_COUNT, ATTENTION_HEADS, HEAD_CHANNELS)
        gate_values = alignment_row[:, 3 * feature_width:].astype(jnp.float32)
        scores = jnp.einsum('ihd,jhd->hij', query_rows, key_rows) / jnp.sqrt(jnp.float32(HEAD_CHANNELS)) + bias
        scores = jnp.where(key_live[None, None, :], scores, jnp.float32(-1000000000.0))
        row_max = lax.optimization_barrier(jnp.max(scores, axis=-1, keepdims=True))
        expo = jnp.exp(scores - row_max)
        weights = (expo / lax.optimization_barrier(jnp.sum(expo, axis=-1, keepdims=True))).astype(jnp.bfloat16)
        attended = jnp.einsum('hij,jhd->ihd', weights.astype(jnp.float32), value_rows).reshape(RESIDUE_COUNT, feature_width)
        gated = (attended * jax.nn.sigmoid(gate_values)).astype(jnp.bfloat16)
        return jnp.dot(gated, mixing_exit_matrix, preferred_element_type=jnp.float32)
    delta_accrued = lax.map(single_row, projected)
    existing_sequences = homolog_live_flags.astype(jnp.float32)
    family_array_reweighted = aligned_family_array + existing_sequences[:, None, None] * delta_accrued
    res_live = amino_real_flags.astype(jnp.float32)
    rescaled_other_operand_z = zscore_elements(family_array_reweighted).astype(jnp.bfloat16)
    factors = jnp.dot(rescaled_other_operand_z.reshape(-1, CM), factor_pair_matrices, preferred_element_type=jnp.float32)
    factors = factors.reshape(ROWS, RESIDUE_COUNT, 2 * OPM) * (existing_sequences[:, None] * res_live[None, :])[:, :, None]
    factors = factors.astype(jnp.bfloat16)
    left = factors[:, :, :OPM].astype(jnp.float32)
    right = factors[:, :, OPM:].astype(jnp.float32)

    def block(first):
        left_block = lax.dynamic_slice_in_dim(left, first, RES_DEV, 1)
        outer = jnp.einsum('sic,sje->ijce', left_block, right).reshape(RES_DEV, RESIDUE_COUNT, OPM * OPM)
        return jnp.einsum('ijk,kz->ijz', outer, tensor_mean_matrix, precision=lax.Precision.HIGHEST)
    starts = (jnp.arange(N_RES) * RES_DEV).astype(jnp.int32)
    projection = lax.map(block, starts).reshape(RESIDUE_COUNT, RESIDUE_COUNT, CZ)
    live_rows = jnp.sum(existing_sequences)
    norm = jnp.maximum(live_rows * res_live[:, None] * res_live[None, :], 1.0)
    contact_grid_result = couple_representation + projection / norm[:, :, None]
    return (family_array_reweighted, contact_grid_result)
```

```python
import functools
import math

import jax
import jax.numpy as jnp
from jax import lax
from jax.experimental import pallas as pl
from jax.experimental.pallas import tpu as pltpu
from jax.sharding import PartitionSpec as P

MESH = pl.DeviceIdType.MESH
F32 = jnp.float32
BF16 = jnp.bfloat16
LOG2E = math.log2(math.e)
VMEM_LIMIT = 56 * 1024 * 1024

N_RES, N_SEQ = 32, 4
S_LOC, I_LOC, J_LOC = 32, 24, 192
CM, CZ, HEADS, HD, OPM = 256, 128, 8, 32, 32
RES = 768
GROUPS = 4
ROWS_PER = 8


def lane_iota(shape):
    return lax.broadcasted_iota(jnp.int32, shape, len(shape) - 1)


def layer_norm(x):
    centre = jnp.mean(x, axis=-1, keepdims=True)
    d = x - centre
    spread = jnp.mean(d * d, axis=-1, keepdims=True)
    return d * lax.rsqrt(spread + 1e-05)


def project_kernel(msa, w, pair, wshift, qkvg, bias):
    s = lax.axis_index("seq")
    normed = layer_norm(msa[...].reshape(S_LOC * I_LOC, CM)).astype(BF16)
    lane = lane_iota((CM, 128))
    lane_o = lane_iota((S_LOC * I_LOC, 128))
    scale = jnp.where(lane_o < HD, F32(LOG2E / math.sqrt(HD)), F32(1.0))
    for h in range(HEADS):
        wh = None
        for part in range(4):
            col = part * 256 + (h // 4) * 128
            piece = w[:, col : col + 128].astype(F32)
            shift = (part * 32 - (h % 4) * 32) % 128
            if shift:
                piece = pltpu.roll(piece, shift, 1)
            wh = piece if wh is None else jnp.where(lane >= part * 32, piece, wh)
        out = jnp.dot(normed, wh.astype(BF16), preferred_element_type=F32) * scale
        qkvg[h] = out.astype(BF16).reshape(GROUPS, ROWS_PER, I_LOC, 128)
    odd = s % 2
    chunk = 4
    for i0 in range(0, I_LOC, chunk):
        z = layer_norm(pair[i0 : i0 + chunk].reshape(chunk * J_LOC, CZ))
        b = lax.dot_general(
            wshift[...],
            z,
            (((0,), (1,)), ((), ())),
            precision=lax.Precision.HIGHEST,
            preferred_element_type=F32,
        )
        for i in range(chunk):
            row = b[:, i * J_LOC : (i + 1) * J_LOC]
            bias[i0 + i] = row


def project(msa, w, pair, wshift):
    return pl.pallas_call(
        project_kernel,
        out_shape=(
            jax.ShapeDtypeStruct((HEADS, GROUPS, ROWS_PER, I_LOC, 128), BF16),
            jax.ShapeDtypeStruct((I_LOC, HEADS, J_LOC), F32),
        ),
        in_specs=[pl.BlockSpec(memory_space=pltpu.VMEM)] * 4,
        out_specs=(pl.BlockSpec(memory_space=pltpu.VMEM),) * 2,
        compiler_params=pltpu.CompilerParams(vmem_limit_bytes=VMEM_LIMIT),
        name="project",
    )(msa, w, pair, wshift)


def offset(k, r):
    kk = lax.rem(k * 11, N_RES)
    x = lax.rem(lax.div(r, 8) + lax.div(kk, 8), 4)
    y = lax.rem(lax.div(r, 4) + lax.div(kk, 4), 2)
    z = lax.rem(r + kk, 4)
    return x * 8 + y * 4 + z


def attend_kernel(
    qkvg, bias_in, poly_col, poly_row, amino_col, amino_row, shifts,
    back,
    recv, b1, br, bias, acc, ret,
    ss, rs, s1, r1, s2, r2, s3, r3, sb, rb, loc,
):
    r, s = lax.axis_index("res"), lax.axis_index("seq")
    h, z = lax.div(r, 4), lax.rem(r, 4)
    s_y = lax.rem(s + 2, 4)
    s_c = s + 1 - 2 * lax.rem(s, 2)

    def remote(src, dst, a, b, d, q):
        return pltpu.make_async_remote_copy(
            src_ref=src, dst_ref=dst, send_sem=a, recv_sem=b, device_id=(d, q), device_id_type=MESH
        )

    barrier = pltpu.get_barrier_semaphore()

    def greet(k, c):
        pl.semaphore_signal(barrier, inc=1, device_id=(offset(k, r), s), device_id_type=MESH)
        return c

    lax.fori_loop(1, N_RES, greet, 0)

    def greet_y(k, c):
        pl.semaphore_signal(barrier, inc=1, device_id=(h * 4 + k, s_y), device_id_type=MESH)
        return c

    lax.fori_loop(0, 4, greet_y, 0)
    pl.semaphore_signal(barrier, inc=1, device_id=(r, s_c), device_id_type=MESH)
    own = pltpu.make_async_copy(qkvg.at[r], recv.at[r], loc.at[0])
    own.start()
    own1 = pltpu.make_async_copy(bias_in.at[h], b1.at[h], loc.at[1])
    own1.start()
    pl.semaphore_wait(barrier, 36)

    def send1(k, c):
        hh = lax.rem(h + k, 8)
        remote(bias_in.at[hh], b1.at[h], s1.at[hh], r1.at[h], hh * 4 + z, s).start()
        return c

    lax.fori_loop(1, 8, send1, 0)

    def send(k, c):
        d = offset(k, r)
        remote(qkvg.at[d], recv.at[r], ss.at[d], rs.at[r], d, s).start()
        return c

    lax.fori_loop(1, N_RES, send, 0)

    def wait1(k, c):
        hh = lax.rem(h + k, 8)
        cp = remote(bias_in.at[hh], b1.at[hh], s1.at[hh], r1.at[hh], hh * 4 + z, s)
        cp.wait_send()
        cp.wait_recv()
        return c

    lax.fori_loop(1, 8, wait1, 0)
    own1.wait()
    own2 = pltpu.make_async_copy(b1, br.at[s, z], loc.at[2])
    own2.start()

    def send2(k, c):
        zz = lax.rem(z + k, 4)
        q = lax.rem(s + 2 * lax.div(k, 4), 4)
        remote(b1, br.at[s, z], s2.at[k], r2.at[lax.div(s, 2) * 4 + z], h * 4 + zz, q).start()
        return c

    lax.fori_loop(1, 8, send2, 0)

    def wait2(k, c):
        zz = lax.rem(z + k, 4)
        q = lax.rem(s + 2 * lax.div(k, 4), 4)
        cp = remote(b1, br.at[q, zz], s2.at[k], r2.at[lax.div(q, 2) * 4 + zz], h * 4 + zz, q)
        cp.wait_send()
        cp.wait_recv()
        return c

    lax.fori_loop(1, 8, wait2, 0)
    own2.wait()
    for t in range(2):
        q = lax.rem(s + 2 * t, 4)
        remote(br.at[q], br.at[q], s3.at[lax.div(q, 2)], r3.at[lax.div(q, 2)], r, s_c).start()

    def wait_in(k, c):
        d = offset(k, r)
        cp = remote(qkvg.at[d], recv.at[d], ss.at[d], rs.at[d], d, s)
        cp.wait_send()
        cp.wait_recv()
        return c

    lax.fori_loop(1, N_RES, wait_in, 0)
    own.wait()
    for t in range(2):
        q = lax.rem(s + 2 * t, 4)
        qc = q + 1 - 2 * lax.rem(q, 2)
        cp = remote(br.at[qc], br.at[qc], s3.at[lax.div(q, 2)], r3.at[lax.div(q, 2)], r, s_c)
        cp.wait_send()
        cp.wait_recv()

    shift = shifts[h]
    lane24 = lane_iota((I_LOC, 128))

    def build(k, c):
        zz, hh = lax.rem(k, 4), lax.div(k, 4)
        row = pl.multiple_of(k * I_LOC, 8)
        mine = poly_col[pl.ds(row, I_LOC), :]
        t = [br[q, zz, hh].astype(F32) for q in range(4)]
        tiles = [
            t[0][:, :128],
            jnp.where(lane24 < 64, t[0][:, 128:], t[1][:, :128]),
            t[1][:, 128:],
            t[2][:, :128],
            jnp.where(lane24 < 64, t[2][:, 128:], t[3][:, :128]),
            t[3][:, 128:],
        ]
        for n in range(6):
            cols = slice(n * 128, (n + 1) * 128)
            full = tiles[n] + jnp.where(mine != poly_row[:, cols], shift, F32(0.0))
            full = jnp.where(amino_row[:, cols] > 0, full * F32(LOG2E), F32(-1e9))
            bias[pl.ds(row, I_LOC), cols] = full
        return c

    lax.fori_loop(0, N_RES, build, 0)
    acc[...] = jnp.zeros_like(acc)
    lane = lane_iota((RES, 128))
    alive = amino_col[...] > 0

    def one_row(rr, c):
        x = recv[:, rr].astype(F32).reshape(RES, 128)
        xq = jnp.where(lane < HD, x, F32(0.0)).astype(BF16)
        turned = pltpu.roll(x, 96, 1)
        xk = jnp.where(alive, turned, F32(0.0)).astype(BF16)
        xv = jnp.where((lane >= 64) & (lane < 96), x, F32(1.0)).astype(BF16)
        gate = jax.nn.sigmoid(turned)
        slot = lax.rem(rr, 4) * HD
        for q0 in range(0, RES, 256):
            rows = slice(q0, q0 + 256)
            sc = lax.dot_general(
                xq[rows], xk, (((1,), (1,)), ((), ())), preferred_element_type=F32
            )
            sc = sc + bias[rows, :]
            m = jnp.max(sc, axis=-1, keepdims=True)
            p = jnp.exp2(sc - m).astype(BF16)
            o = jnp.dot(p, xv, preferred_element_type=F32)
            o = o / pltpu.roll(o, 64, 1) * gate[rows]
            o = pltpu.roll(o, lax.rem(slot + 64, 128), 1)
            ln = lane[rows]
            keep = (ln >= slot) & (ln < slot + HD)
            acc[lax.div(rr, 4), rows, :] += jnp.where(keep, o, F32(0.0))
        return c

    lax.fori_loop(0, ROWS_PER, one_row, 0)
    for half in range(2):
        ret[:, half] = acc[half].reshape(N_RES, I_LOC, 128).astype(BF16)

    ownb = pltpu.make_async_copy(ret.at[r], back.at[r], loc.at[3])
    ownb.start()

    def send_back(k, c):
        d = offset(k, r)
        remote(ret.at[d], back.at[r], sb.at[d], rb.at[r], d, s).start()
        return c

    lax.fori_loop(1, N_RES, send_back, 0)

    def wait_back(k, c):
        d = offset(k, r)
        cp = remote(ret.at[d], back.at[d], sb.at[d], rb.at[d], d, s)
        cp.wait_send()
        cp.wait_recv()
        return c

    lax.fori_loop(1, N_RES, wait_back, 0)
    ownb.wait()


def attend(qkvg, bias_in, poly, amino, shifts):
    dma = pltpu.SemaphoreType.DMA
    vm = pl.BlockSpec(memory_space=pltpu.VMEM)
    return pl.pallas_call(
        attend_kernel,
        out_shape=jax.ShapeDtypeStruct((N_RES, 2, I_LOC, 128), BF16),
        in_specs=[vm] * 6 + [pl.BlockSpec(memory_space=pltpu.SMEM)],
        out_specs=vm,
        scratch_shapes=[
            pltpu.VMEM((N_RES, ROWS_PER, I_LOC, 128), BF16),
            pltpu.VMEM((HEADS, I_LOC, 256), BF16),
            pltpu.VMEM((N_SEQ, 4, HEADS, I_LOC, 256), BF16),
            pltpu.VMEM((RES, RES), F32),
            pltpu.VMEM((2, RES, 128), F32),
            pltpu.VMEM((N_RES, 2, I_LOC, 128), BF16),
            dma((N_RES,)), dma((N_RES,)), dma((8,)), dma((8,)), dma((8,)), dma((8,)),
            dma((2,)), dma((2,)), dma((N_RES,)), dma((N_RES,)), dma((4,)),
        ],
        compiler_params=pltpu.CompilerParams(
            collective_id=0, has_side_effects=True, vmem_limit_bytes=VMEM_LIMIT
        ),
        name="attend",
    )(qkvg, bias_in, poly[:, None], poly[None, :], amino[:, None], amino[None, :], shifts)


J_CHUNK = 4


def outer_kernel(
    back, msa, pair, wmix, wfac, tmat, amino_col, live,
    family, contact,
    bd_mix, fac, tr, lbuf, rbuf, lall, rall, bd, tcat, lhs, amat,
    sl, rl, sr, rr_sem, loc,
):
    r, s = lax.axis_index("res"), lax.axis_index("seq")
    b, mine = lax.div(r, 8), lax.rem(r, 8) * 4 + s
    holds = b == s

    def remote(src, dst, a, bb, d, q):
        return pltpu.make_async_remote_copy(
            src_ref=src, dst_ref=dst, send_sem=a, recv_sem=bb, device_id=(d, q), device_id_type=MESH
        )

    def source(k):
        return 8 * s + lax.div(k, 4), lax.rem(k, 4)

    barrier = pltpu.get_barrier_semaphore()

    def greet(k, c):
        rr, q = source(k)

        @pl.when(jnp.logical_or(rr != r, q != s))
        def _():
            pl.semaphore_signal(barrier, inc=1, device_id=(rr, q), device_id_type=MESH)

        return c

    lax.fori_loop(0, N_RES, greet, 0)

    def greet_seq(k, c):
        pl.semaphore_signal(barrier, inc=1, device_id=(r, lax.rem(s + k, 4)), device_id_type=MESH)
        return c

    lax.fori_loop(1, N_SEQ, greet_seq, 0)

    bd_mix[...] = jnp.zeros_like(bd_mix)
    for h in range(HEADS):
        for k in range(4):
            bd_mix[h * 128 + k * 32 : h * 128 + (k + 1) * 32, k * CM : (k + 1) * CM] = wmix[
                h * HD : (h + 1) * HD, :
            ]
    gated = jnp.concatenate(
        [back[4 * h : 4 * h + 4].astype(F32).reshape(8 * I_LOC, 128) for h in range(HEADS)], axis=1
    ).astype(BF16)
    own_live = amino_col[pl.ds(pl.multiple_of(r * I_LOC, 8), I_LOC), :].astype(F32)
    for k in range(4):
        delta = jnp.dot(
            gated, bd_mix[:, k * CM : (k + 1) * CM], preferred_element_type=F32
        ).reshape(8, I_LOC, CM)
        for g in range(8):
            row = g * 4 + k
            on = live[s * S_LOC + row].astype(F32)
            fam = msa[row] + on * delta[g]
            family[row] = fam
            f = jnp.dot(layer_norm(fam).astype(BF16), wfac[...], preferred_element_type=F32)
            fac[row * I_LOC : (row + 1) * I_LOC, :] = jnp.concatenate(
                [f * (on * own_live), jnp.zeros((I_LOC, 64), F32)], axis=1
            )
    lane32 = lane_iota((S_LOC, 128))
    for i0 in range(0, I_LOC, 4):
        tile = jnp.zeros((S_LOC, 128), F32)
        for k in range(4):
            i = i0 + k
            f = fac[pl.ds(i, S_LOC, stride=I_LOC), :]
            moved = pltpu.roll(f, k * 32, 1) if k else f
            tile = jnp.where((lane32 >= k * 32) & (lane32 < (k + 1) * 32), moved, tile)
            ft = jnp.transpose(f, (1, 0))[OPM : 2 * OPM, :]
            tr[i * OPM : (i + 1) * OPM, :] = jnp.concatenate(
                [ft, jnp.zeros((OPM, 128 - S_LOC), F32)], axis=1
            )
        lbuf[:, i0 * 32 : (i0 + 4) * 32] = tile.astype(BF16)
    lane24 = lane_iota((I_LOC, 128))
    for e0 in range(0, OPM, 4):
        tile = tr[pl.ds(e0, I_LOC, stride=OPM), :]
        for k in range(1, 4):
            moved = pltpu.roll(tr[pl.ds(e0 + k, I_LOC, stride=OPM), :], k * 32, 1)
            tile = jnp.where((lane24 >= k * 32) & (lane24 < (k + 1) * 32), moved, tile)
        rbuf[:, e0 * 32 : (e0 + 4) * 32] = tile.astype(BF16)

    pl.semaphore_wait(barrier, N_RES - holds.astype(jnp.int32) + 3)

    def send_left(k, c):
        q = lax.rem(s + k, 4)
        remote(lbuf, lall.at[s], sl.at[q], rl.at[s], r, q).start()
        return c

    lax.fori_loop(1, N_SEQ, send_left, 0)

    def send_right(k, c):
        d = offset(k, r)

        @pl.when(jnp.logical_or(k != 0, jnp.logical_not(holds)))
        def _():
            remote(rbuf, rall.at[mine], sr.at[d], rr_sem.at[mine], d, b).start()

        return c

    lax.fori_loop(0, N_RES, send_right, 0)
    ownl = pltpu.make_async_copy(lbuf, lall.at[s], loc.at[0])
    ownl.start()

    @pl.when(holds)
    def _():
        cp = pltpu.make_async_copy(rbuf, rall.at[mine], loc.at[1])
        cp.start()
        cp.wait()

    for e in range(OPM):
        t = tmat[pl.ds(e, OPM, stride=OPM), :]
        head = t.astype(BF16)
        tcat[e * 32 : (e + 1) * 32, 0:128] = head
        tcat[e * 32 : (e + 1) * 32, 128:256] = (t - head.astype(F32)).astype(BF16)

    def wait_left(k, c):
        q = lax.rem(s + k, 4)
        cp = remote(lbuf, lall.at[q], sl.at[q], rl.at[q], r, q)
        cp.wait_send()
        cp.wait_recv()
        return c

    lax.fori_loop(1, N_SEQ, wait_left, 0)
    ownl.wait()
    sel_r = lax.broadcasted_iota(jnp.int32, (128, 512), 0)
    sel_c = lax.broadcasted_iota(jnp.int32, (128, 512), 1)
    same = (lax.div(sel_r, 32) == lax.div(sel_c, 128)) & (lax.rem(sel_r, 32) == lax.rem(sel_c, 32))
    sel = jnp.where(same, F32(1.0), F32(0.0)).astype(BF16)
    for i0 in range(0, I_LOC, 4):
        for q in range(N_SEQ):
            rep = jnp.dot(lall[q, :, i0 * 32 : (i0 + 4) * 32], sel, preferred_element_type=F32)
            for k in range(4):
                i = i0 + k
                piece = rep[:, k * 128 : (k + 1) * 128]
                for e in range(4):
                    keep = (lane32 >= e * 32) & (lane32 < (e + 1) * 32)
                    bd[
                        i // 2,
                        q * 128 + e * 32 : q * 128 + (e + 1) * 32,
                        (i % 2) * 128 : (i % 2 + 1) * 128,
                    ] = jnp.where(keep, piece, F32(0.0)).astype(BF16)

    count = lax.fori_loop(
        0, 128, lambda k, c: c + live[k], jnp.int32(0)
    ).astype(F32)
    inv = 1.0 / jnp.maximum(jnp.full((1, 128), count, F32), 1.0)

    def wait_right(k, c):
        rr, q = source(k)

        @pl.when(jnp.logical_or(rr != r, q != s))
        def _():
            remote(rbuf, rall.at[k], sr.at[k], rr_sem.at[k], rr, q).wait_recv()

        return c

    jc = J_CHUNK * I_LOC
    for c0 in range(0, 8, J_CHUNK):
        lax.fori_loop(4 * c0, 4 * (c0 + J_CHUNK), wait_right, 0)
        for q in range(N_SEQ):
            for g in range(8):
                cols = slice(g * 128, (g + 1) * 128)
                rows = jnp.concatenate(
                    [rall[4 * (c0 + t) + q, :, cols].astype(F32) for t in range(J_CHUNK)], axis=0
                )
                lhs[g * jc : (g + 1) * jc, q * 128 : (q + 1) * 128] = rows.astype(BF16)

        def pair_of(p, c):
            a = jnp.dot(lhs[...], bd[p], preferred_element_type=F32).astype(BF16)
            for half in range(2):
                for g in range(8):
                    amat[2 * p + half, :, g * 128 : (g + 1) * 128] = a[
                        g * jc : (g + 1) * jc, half * 128 : (half + 1) * 128
                    ]
            return c

        lax.fori_loop(0, I_LOC // 2, pair_of, 0)

        def finish(p, c):
            am = amat[pl.ds(4 * p, 4)].reshape(4 * jc, 1024)
            o = jnp.dot(am, tcat[...], preferred_element_type=F32)
            o = (o[:, :128] + o[:, 128:]) * inv
            where = (pl.ds(4 * p, 4), pl.ds(c0 * I_LOC, jc))
            contact[where] = pair[where] + o.reshape(4, jc, CZ)
            return c

        lax.fori_loop(0, I_LOC // 4, finish, 0)

    def wait_sent(k, c):
        @pl.when(jnp.logical_or(k != r, jnp.logical_not(holds)))
        def _():
            remote(rbuf, rall.at[k], sr.at[k], rr_sem.at[k], k, b).wait_send()

        return c

    lax.fori_loop(0, N_RES, wait_sent, 0)


def outer(back, msa, pair, wmix, wfac, tmat, amino, live):
    dma = pltpu.SemaphoreType.DMA
    vm = pl.BlockSpec(memory_space=pltpu.VMEM)
    jc = J_CHUNK * I_LOC
    return pl.pallas_call(
        outer_kernel,
        out_shape=(
            jax.ShapeDtypeStruct((S_LOC, I_LOC, CM), F32),
            jax.ShapeDtypeStruct((I_LOC, J_LOC, CZ), F32),
        ),
        in_specs=[vm] * 7 + [pl.BlockSpec(memory_space=pltpu.SMEM)],
        out_specs=(vm, vm),
        scratch_shapes=[
            pltpu.VMEM((1024, 1024), BF16),
            pltpu.VMEM((S_LOC * I_LOC, 128), F32),
            pltpu.VMEM((I_LOC * OPM, 128), F32),
            pltpu.VMEM((S_LOC, I_LOC * OPM), BF16),
            pltpu.VMEM((I_LOC, OPM * S_LOC), BF16),
            pltpu.VMEM((N_SEQ, S_LOC, I_LOC * OPM), BF16),
            pltpu.VMEM((N_RES, I_LOC, OPM * S_LOC), BF16),
            pltpu.VMEM((I_LOC // 2, 512, 256), BF16),
            pltpu.VMEM((1024, 256), BF16),
            pltpu.VMEM((8 * jc, 512), BF16),
            pltpu.VMEM((I_LOC, jc, 1024), BF16),
            dma((4,)), dma((4,)), dma((N_RES,)), dma((N_RES,)), dma((2,)),
        ],
        compiler_params=pltpu.CompilerParams(
            collective_id=1, has_side_effects=True, vmem_limit_bytes=VMEM_LIMIT
        ),
        name="outer",
    )(back, msa, pair, wmix, wfac, tmat, amino[:, None], live)


def on_device(msa, pair, amino, poly, live, w, wshift, shifts, wmix, wfac, tmat):
    qkvg, bias = project(msa, w, pair, wshift)
    qkvg = qkvg.reshape(N_RES, ROWS_PER, I_LOC, 128)
    bias = jnp.transpose(bias, (1, 0, 2)).astype(BF16)
    low = jnp.pad(bias, ((0, 0), (0, 0), (0, 64)))
    high = jnp.pad(bias, ((0, 0), (0, 0), (64, 0)))
    bias = jnp.where(lax.axis_index("seq") % 2 == 0, low, high)
    back = attend(qkvg, bias, poly, amino, shifts)
    return outer(back, msa, pair, wmix, wfac, tmat, amino, live)


def solution(mesh):
    in_specs = (P("seq", "res", None), P("res", "seq", None)) + (P(),) * 9
    out_specs = (P("seq", "res", None), P("res", "seq", None))
    return jax.shard_map(
        on_device, mesh=mesh, in_specs=in_specs, out_specs=out_specs, check_vma=False
    )
```

```python
import math

import jax
import jax.numpy as jnp
from jax import lax
from jax.experimental import pallas as pl
from jax.experimental.pallas import tpu as pltpu
from jax.sharding import PartitionSpec as P

MESH = pl.DeviceIdType.MESH
F32 = jnp.float32
BF16 = jnp.bfloat16
LOG2E = math.log2(math.e)
VMEM_LIMIT = 58 * 1024 * 1024

N_RES, N_SEQ = 32, 4
S_LOC, I_LOC, J_LOC = 32, 24, 192
CM, CZ, HEADS, HD, OPM = 256, 128, 8, 32, 32
RES = 768
Q_CHUNK = 256
J_BLOCKS = 2
JC = J_BLOCKS * I_LOC


def lane_iota(shape):
    return lax.broadcasted_iota(jnp.int32, shape, len(shape) - 1)


def in_slot(lane, k):
    return (lane >= k * 32) & (lane < (k + 1) * 32)


def layer_norm(x):
    centre = jnp.mean(x, axis=-1, keepdims=True)
    d = x - centre
    spread = jnp.mean(d * d, axis=-1, keepdims=True)
    return d * lax.rsqrt(spread + 1e-05)


def nt_dot(a, b, precision=None):
    return lax.dot_general(
        a, b, (((1,), (1,)), ((), ())), precision=precision, preferred_element_type=F32
    )


def offset(k, r):
    kk = lax.rem(k * 11, N_RES)
    x = lax.rem(lax.div(r, 8) + lax.div(kk, 8), 4)
    y = lax.rem(lax.div(r, 4) + lax.div(kk, 4), 2)
    z = lax.rem(r + kk, 4)
    return x * 8 + y * 4 + z


def remote(src, dst, a, b, d, q):
    return pltpu.make_async_remote_copy(
        src_ref=src, dst_ref=dst, send_sem=a, recv_sem=b, device_id=(d, q), device_id_type=MESH
    )


def kernel(
    msa, pair, amino, poly, w, wshift_t, wmix, wfac_t, tmat, live, shifts,
    family, contact,
    btmp, bsend, b1, br, bias, pgate, gate, qsend, recv, qs, ks, vs, acc, ret, back,
    bd_mix, fac, tr, lbuf, rbuf, lall, rall, bd, tcat, lhs, amat,
    ss, rs, s1, r1, s2, r2, s3, r3, sb, rb, sl, rl, sr, rr_sem, loc, locb,
):
    r, s = lax.axis_index("res"), lax.axis_index("seq")
    h, z = lax.div(r, 4), lax.rem(r, 4)
    y_lo = lax.rem(h, 2)
    s_y = lax.rem(s + 2, 4)
    s_c = s + 1 - 2 * lax.rem(s, 2)
    b, mine = lax.div(r, 8), lax.rem(r, 8) * 4 + s
    holds = b == s

    def source(k):
        return 8 * s + lax.div(k, 4), lax.rem(k, 4)

    barrier = pltpu.get_barrier_semaphore()

    def greet(k, c):
        pl.semaphore_signal(barrier, inc=1, device_id=(offset(k, r), s), device_id_type=MESH)
        return c

    lax.fori_loop(1, N_RES, greet, 0)

    def greet_y(k, c):
        pl.semaphore_signal(barrier, inc=1, device_id=(h * 4 + k, s_y), device_id_type=MESH)
        return c

    lax.fori_loop(0, 4, greet_y, 0)

    def greet_seq(k, c):
        pl.semaphore_signal(barrier, inc=1, device_id=(r, lax.rem(s + k, 4)), device_id_type=MESH)
        return c

    lax.fori_loop(1, N_SEQ, greet_seq, 0)

    def greet_right(k, c):
        rr, q = source(k)

        @pl.when(jnp.logical_or(rr != r, q != s))
        def _():
            pl.semaphore_signal(barrier, inc=1, device_id=(rr, q), device_id_type=MESH)

        return c

    lax.fori_loop(0, N_RES, greet_right, 0)

    btmp[...] = jnp.zeros_like(btmp)
    chunk = 4
    for i0 in range(0, I_LOC, chunk):
        zn = layer_norm(pair[i0 : i0 + chunk].reshape(chunk * J_LOC, CZ))
        bb = nt_dot(wshift_t[...], zn, lax.Precision.HIGHEST)
        for i in range(chunk):
            rows, col = slice((i0 + i) * HEADS, (i0 + i + 1) * HEADS), i * J_LOC
            btmp[0, rows, :] = bb[:, col : col + 128]
            btmp[1, rows, 0:64] = bb[:, col + 128 : col + J_LOC]
    odd = jnp.full((I_LOC, 256), lax.rem(s, 2), jnp.int32) > 0
    for hh in range(HEADS):
        v = jnp.concatenate(
            [btmp[n, pl.ds(hh, I_LOC, stride=HEADS), :] for n in range(2)], axis=1
        )
        bsend[hh] = jnp.where(odd, pltpu.roll(v, 64, 1), v).astype(BF16)

    pl.semaphore_wait(barrier, 31 + 4 + 3 + N_RES - holds.astype(jnp.int32))

    own1 = pltpu.make_async_copy(bsend.at[h], b1.at[h], loc.at[1])
    own1.start()

    def send1(k, c):
        hh = lax.rem(h + k, 8)
        remote(bsend.at[hh], b1.at[h], s1.at[hh], r1.at[h], hh * 4 + z, s).start()
        return c

    lax.fori_loop(1, 8, send1, 0)

    normed = layer_norm(msa[...].reshape(S_LOC * I_LOC, CM)).astype(BF16)
    lane3 = lane_iota((8, I_LOC, 128))
    for part in range(3):
        out = jnp.dot(normed, w[:, part * CM : (part + 1) * CM], preferred_element_type=F32)
        if part == 0:
            out = out * F32(LOG2E / math.sqrt(HD))
        for t in range(2):
            cols = out[:, t * 128 : (t + 1) * 128].reshape(8, 4, I_LOC, 128)
            for a in range(4):
                tile = None
                for k in range(4):
                    piece = cols[:, k]
                    if (k - a) % 4:
                        piece = pltpu.roll(piece, (k - a) % 4 * 32, 2)
                    tile = piece if tile is None else jnp.where(in_slot(lane3, k), piece, tile)
                tile = tile.astype(BF16)
                for g in range(4):
                    for half in range(2):
                        qsend[(t * 4 + a) * 4 + g, half, part] = tile[g * 2 + half]

    def wait1(k, c):
        hh = lax.rem(h + k, 8)
        remote(bsend.at[hh], b1.at[hh], s1.at[hh], r1.at[hh], hh * 4 + z, s).wait_recv()
        return c

    lax.fori_loop(1, 8, wait1, 0)
    own1.wait()
    own2 = pltpu.make_async_copy(b1, br.at[s, z], loc.at[2])
    own2.start()

    def send2(k, c):
        zz = lax.rem(z + k, 4)
        q = lax.rem(s + 2 * lax.div(k, 4), 4)
        remote(b1, br.at[s, z], s2.at[k], r2.at[lax.div(s, 2) * 4 + z], h * 4 + zz, q).start()
        return c

    lax.fori_loop(1, 8, send2, 0)

    for half in range(2):
        pltpu.make_async_copy(qsend.at[r, half], recv.at[half, r], locb.at[half]).start()

        def send(k, c, half=half):
            d = offset(k, r)
            remote(qsend.at[d, half], recv.at[half, r], ss.at[half, d], rs.at[half, r], d, s).start()
            return c

        lax.fori_loop(1, N_RES, send, 0)

    pgate[...] = jnp.dot(normed, w[:, 3 * CM :], preferred_element_type=F32).astype(BF16).astype(F32)
    for t in range(2):
        cols = jax.nn.sigmoid(pgate[:, t * 128 : (t + 1) * 128]).reshape(8, 4, I_LOC, 128)
        for a in range(4):
            tile = None
            for k in range(4):
                piece = cols[:, k]
                if (k - a) % 4:
                    piece = pltpu.roll(piece, (k - a) % 4 * 32, 2)
                tile = piece if tile is None else jnp.where(in_slot(lane3, k), piece, tile)
            for g in range(4):
                for half in range(2):
                    gate[half, t * 4 + a, g] = tile[g * 2 + half]
    bd_mix[...] = jnp.zeros_like(bd_mix)
    for hh in range(HEADS):
        for k in range(4):
            bd_mix[hh * 128 + k * 32 : hh * 128 + (k + 1) * 32, k * CM : (k + 1) * CM] = wmix[
                hh * HD : (hh + 1) * HD, :
            ]
    for e in range(OPM):
        t = tmat[pl.ds(e, OPM, stride=OPM), :]
        head = t.astype(BF16)
        tcat[e * 32 : (e + 1) * 32, 0:128] = head
        tcat[e * 32 : (e + 1) * 32, 128:256] = (t - head.astype(F32)).astype(BF16)
    acc[...] = jnp.zeros_like(acc)
    amino_row = amino[...].reshape(1, RES)
    poly_row = poly[...].reshape(1, RES)

    def column(row, n):
        tile = row[:, n * 128 : (n + 1) * 128].astype(F32)
        return jnp.transpose(jnp.broadcast_to(tile, (128, 128)), (1, 0))

    amino_col = [column(amino_row, n) for n in range(6)]
    for n in range(6):
        fac[n * 128 : (n + 1) * 128, :] = column(poly_row, n)

    def wait2(k, c):
        zz = lax.rem(z + k, 4)
        q = lax.rem(s + 2 * lax.div(k, 4), 4)
        remote(b1, br.at[q, zz], s2.at[k], r2.at[lax.div(q, 2) * 4 + zz], h * 4 + zz, q).wait_recv()
        return c

    lax.fori_loop(1, 8, wait2, 0)
    own2.wait()
    for t in range(2):
        q = lax.rem(s + 2 * t, 4)
        remote(br.at[q], br.at[q], s3.at[lax.div(q, 2)], r3.at[lax.div(q, 2)], r, s_c).start()
    for t in range(2):
        q = lax.rem(s + 2 * t, 4)
        qc = q + 1 - 2 * lax.rem(q, 2)
        remote(br.at[qc], br.at[qc], s3.at[lax.div(q, 2)], r3.at[lax.div(q, 2)], r, s_c).wait_recv()

    shift = shifts[h]
    lane24 = lane_iota((I_LOC, 128))
    poly_f = poly_row.astype(F32)

    def build(k, c):
        zz, hh = lax.rem(k, 4), lax.div(k, 4)
        row = pl.multiple_of(k * I_LOC, 8)
        own = fac[pl.ds(row, I_LOC), :]
        t = [br[q, zz, hh].astype(F32) for q in range(4)]
        tiles = [
            t[0][:, :128],
            jnp.where(lane24 < 64, t[0][:, 128:], t[1][:, :128]),
            t[1][:, 128:],
            t[2][:, :128],
            jnp.where(lane24 < 64, t[2][:, 128:], t[3][:, :128]),
            t[3][:, 128:],
        ]
        for n in range(6):
            cols = slice(n * 128, (n + 1) * 128)
            full = tiles[n] + jnp.where(own != poly_f[:, cols], shift, F32(0.0))
            full = jnp.where(amino_row[:, cols] > 0, full * F32(LOG2E), F32(-1e9))
            bias[pl.ds(row, I_LOC), cols] = full
        return c

    lax.fori_loop(0, N_RES, build, 0)

    lane_q = lane_iota((Q_CHUNK, 128))
    lane = lane_iota((RES, 128))
    for half in range(2):

        def wait_in(k, c, half=half):
            d = offset(k, r)
            remote(
                qsend.at[d, half], recv.at[half, d], ss.at[half, d], rs.at[half, d], d, s
            ).wait_recv()
            return c

        lax.fori_loop(1, N_RES, wait_in, 0)
        pltpu.make_async_copy(qsend.at[r, half], recv.at[half, r], locb.at[half]).wait()
        qs[...] = recv[half, :, 0].astype(F32).reshape(RES, 128).astype(BF16)
        kf = recv[half, :, 1].astype(F32).reshape(RES, 128)
        for n in range(6):
            rows = slice(n * 128, (n + 1) * 128)
            ks[rows, :] = jnp.where(amino_col[n] > 0, kf[rows], F32(0.0)).astype(BF16)
        vs[...] = recv[half, :, 2].astype(F32).reshape(RES, 128).astype(BF16)

        def one_row(rr, c, half=half):
            slot = in_slot(lane, rr)
            xv = jnp.where(slot, vs[...].astype(F32), F32(1.0)).astype(BF16)
            xk = ks[...]
            slot_q = in_slot(lane_q, rr)
            for q0 in range(0, RES, Q_CHUNK):
                rows = slice(q0, q0 + Q_CHUNK)
                xq = jnp.where(slot_q, qs[rows, :].astype(F32), F32(0.0)).astype(BF16)
                sc = nt_dot(xq, xk) + bias[rows, :]
                m = jnp.max(sc, axis=-1, keepdims=True)
                p = jnp.exp2(sc - m).astype(BF16)
                o = jnp.dot(p, xv, preferred_element_type=F32)
                o = o / pltpu.roll(o, 32, 1)
                acc[half, rows, :] = jnp.where(slot_q, o, acc[half, rows, :])
            return c

        lax.fori_loop(0, 4, one_row, 0)
        ret[half] = acc[half].reshape(N_RES, I_LOC, 128).astype(BF16)
        pltpu.make_async_copy(ret.at[half, r], back.at[half, r], locb.at[2 + half]).start()

        def send_back(k, c, half=half):
            d = offset(k, r)
            remote(ret.at[half, d], back.at[half, r], sb.at[half, d], rb.at[half, r], d, s).start()
            return c

        lax.fori_loop(1, N_RES, send_back, 0)

    for n in range(6):
        tr[n * 128 : (n + 1) * 128, :] = amino_col[n]
    own_live = tr[pl.ds(pl.multiple_of(r * I_LOC, 8), I_LOC), :]
    for half in range(2):

        def wait_back(k, c, half=half):
            d = offset(k, r)
            remote(
                ret.at[half, d], back.at[half, d], sb.at[half, d], rb.at[half, d], d, s
            ).wait_recv()
            return c

        lax.fori_loop(1, N_RES, wait_back, 0)
        pltpu.make_async_copy(ret.at[half, r], back.at[half, r], locb.at[2 + half]).wait()
        gated = jnp.concatenate(
            [
                (back[half, 4 * hh : 4 * hh + 4].astype(F32) * gate[half, hh]).reshape(4 * I_LOC, 128)
                for hh in range(HEADS)
            ],
            axis=1,
        ).astype(BF16)
        for k in range(4):
            delta = jnp.dot(
                gated, bd_mix[:, k * CM : (k + 1) * CM], preferred_element_type=F32
            ).reshape(4, I_LOC, CM)
            fams = []
            for g in range(4):
                row = g * 8 + half * 4 + k
                fam = msa[row] + live[s * S_LOC + row].astype(F32) * delta[g]
                family[row] = fam
                fams.append(fam)
            y = layer_norm(jnp.concatenate(fams, axis=0)).astype(BF16)
            f = nt_dot(y, wfac_t[...])
            f = jnp.concatenate([f, jnp.zeros((4 * I_LOC, 64), F32)], axis=1)
            for g in range(4):
                row = g * 8 + half * 4 + k
                on = live[s * S_LOC + row].astype(F32)
                fac[row * I_LOC : (row + 1) * I_LOC, :] = f[g * I_LOC : (g + 1) * I_LOC] * (
                    on * own_live
                )

    lane32 = lane_iota((S_LOC, 128))
    for i0 in range(0, I_LOC, 4):
        tile = None
        for k in range(4):
            i = i0 + k
            f = fac[pl.ds(i, S_LOC, stride=I_LOC), :]
            moved = pltpu.roll(f, k * 32, 1) if k else f
            tile = moved if tile is None else jnp.where(in_slot(lane32, k), moved, tile)
            ft = jnp.transpose(f, (1, 0))[OPM : 2 * OPM, :]
            tr[i * OPM : (i + 1) * OPM, :] = jnp.concatenate(
                [ft, jnp.zeros((OPM, 128 - S_LOC), F32)], axis=1
            )
        lbuf[:, i0 * 32 : (i0 + 4) * 32] = tile.astype(BF16)
    for e0 in range(0, OPM, 4):
        tile = tr[pl.ds(e0, I_LOC, stride=OPM), :]
        for k in range(1, 4):
            moved = pltpu.roll(tr[pl.ds(e0 + k, I_LOC, stride=OPM), :], k * 32, 1)
            tile = jnp.where(in_slot(lane24, k), moved, tile)
        rbuf[:, e0 * 32 : (e0 + 4) * 32] = tile.astype(BF16)

    def send_left(k, c):
        q = lax.rem(s + k, 4)
        remote(lbuf, lall.at[s], sl.at[q], rl.at[s], r, q).start()
        return c

    lax.fori_loop(1, N_SEQ, send_left, 0)

    def yz(k):
        kk = lax.rem(k * 3, 8)
        return lax.div(kk, 4), lax.rem(kk, 4)

    def target(k):
        dy, dz = yz(lax.div(k, 4))
        x = lax.rem(b + k, 4)
        return x * 8 + lax.rem(y_lo + dy, 2) * 4 + lax.rem(z + dz, 4)

    def send_right(k, c):
        d = target(k)

        @pl.when(jnp.logical_or(k != 0, jnp.logical_not(holds)))
        def _():
            remote(rbuf, rall.at[mine], sr.at[d], rr_sem.at[mine], d, b).start()

        return c

    lax.fori_loop(0, N_RES, send_right, 0)
    ownl = pltpu.make_async_copy(lbuf, lall.at[s], loc.at[0])
    ownl.start()

    @pl.when(holds)
    def _():
        cp = pltpu.make_async_copy(rbuf, rall.at[mine], loc.at[3])
        cp.start()
        cp.wait()

    def wait_left(k, c):
        q = lax.rem(s + k, 4)
        remote(lbuf, lall.at[q], sl.at[q], rl.at[q], r, q).wait_recv()
        return c

    lax.fori_loop(1, N_SEQ, wait_left, 0)
    ownl.wait()
    sel_r = lax.broadcasted_iota(jnp.int32, (128, 512), 0)
    sel_c = lax.broadcasted_iota(jnp.int32, (128, 512), 1)
    same = (lax.div(sel_r, 32) == lax.div(sel_c, 128)) & (lax.rem(sel_r, 32) == lax.rem(sel_c, 32))
    sel = jnp.where(same, F32(1.0), F32(0.0)).astype(BF16)
    for i0 in range(0, I_LOC, 4):
        for q in range(N_SEQ):
            rep = jnp.dot(lall[q, :, i0 * 32 : (i0 + 4) * 32], sel, preferred_element_type=F32)
            for k in range(4):
                i = i0 + k
                piece = rep[:, k * 128 : (k + 1) * 128]
                for e in range(4):
                    bd[
                        i // 2,
                        q * 128 + e * 32 : q * 128 + (e + 1) * 32,
                        (i % 2) * 128 : (i % 2 + 1) * 128,
                    ] = jnp.where(in_slot(lane32, e), piece, F32(0.0)).astype(BF16)

    count = lax.fori_loop(0, 128, lambda k, c: c + live[k], jnp.int32(0)).astype(F32)
    inv = 1.0 / jnp.maximum(jnp.full((1, 128), count, F32), 1.0)

    for c0 in range(0, 8, J_BLOCKS):
        blocks = []
        for t in range(J_BLOCKS):
            dy, dz = yz(c0 + t)
            blocks.append(lax.rem(y_lo + 2 - dy, 2) * 4 + lax.rem(z + 4 - dz, 4))
        for blk in blocks:

            def wait_right(q, c, blk=blk):
                rr = 8 * s + blk

                @pl.when(jnp.logical_or(rr != r, q != s))
                def _():
                    k = blk * 4 + q
                    remote(rbuf, rall.at[k], sr.at[k], rr_sem.at[k], rr, q).wait_recv()

                return c

            lax.fori_loop(0, N_SEQ, wait_right, 0)
        for q in range(N_SEQ):
            for g in range(8):
                cols = slice(g * 128, (g + 1) * 128)
                rows = jnp.concatenate(
                    [rall[blk * 4 + q, :, cols].astype(F32) for blk in blocks], axis=0
                )
                lhs[g * JC : (g + 1) * JC, q * 128 : (q + 1) * 128] = rows.astype(BF16)

        def pair_of(p, c):
            a = jnp.dot(lhs[...], bd[p], preferred_element_type=F32).astype(BF16)
            for half in range(2):
                for g in range(8):
                    amat[2 * p + half, :, g * 128 : (g + 1) * 128] = a[
                        g * JC : (g + 1) * JC, half * 128 : (half + 1) * 128
                    ]
            return c

        lax.fori_loop(0, I_LOC // 2, pair_of, 0)

        def finish(p, c, blocks=tuple(blocks)):
            am = amat[pl.ds(12 * p, 12)].reshape(12 * JC, 1024)
            o = jnp.dot(am, tcat[...], preferred_element_type=F32)
            o = ((o[:, :128] + o[:, 128:]) * inv).reshape(12, JC, CZ)
            for t, blk in enumerate(blocks):
                at = (pl.ds(12 * p, 12), pl.ds(pl.multiple_of(blk * I_LOC, 8), I_LOC))
                contact[at] = pair[at] + o[:, t * I_LOC : (t + 1) * I_LOC]
            return c

        lax.fori_loop(0, I_LOC // 12, finish, 0)

    def sent1(k, c):
        hh = lax.rem(h + k, 8)
        remote(bsend.at[hh], b1.at[hh], s1.at[hh], r1.at[hh], hh * 4 + z, s).wait_send()
        remote(b1, br.at[s, z], s2.at[k], r2.at[k], r, s_c).wait_send()
        return c

    lax.fori_loop(1, 8, sent1, 0)
    for t in range(2):
        q = lax.rem(s + 2 * t, 4)
        remote(br.at[q], br.at[q], s3.at[lax.div(q, 2)], r3.at[lax.div(q, 2)], r, s_c).wait_send()

    def sent(k, c):
        d = offset(k, r)
        for half in range(2):
            remote(
                qsend.at[d, half], recv.at[half, d], ss.at[half, d], rs.at[half, d], d, s
            ).wait_send()
            remote(
                ret.at[half, d], back.at[half, d], sb.at[half, d], rb.at[half, d], d, s
            ).wait_send()
        return c

    lax.fori_loop(1, N_RES, sent, 0)

    def sent_left(k, c):
        q = lax.rem(s + k, 4)
        remote(lbuf, lall.at[q], sl.at[q], rl.at[q], r, q).wait_send()
        return c

    lax.fori_loop(1, N_SEQ, sent_left, 0)

    def sent_right(k, c):
        @pl.when(jnp.logical_or(k != r, jnp.logical_not(holds)))
        def _():
            remote(rbuf, rall.at[k], sr.at[k], rr_sem.at[k], k, b).wait_send()

        return c

    lax.fori_loop(0, N_RES, sent_right, 0)


def on_device(msa, pair, amino, poly, live, w, wshift, shifts, wmix, wfac, tmat):
    dma = pltpu.SemaphoreType.DMA
    vm = pl.BlockSpec(memory_space=pltpu.VMEM)
    sm = pl.BlockSpec(memory_space=pltpu.SMEM)
    return pl.pallas_call(
        kernel,
        out_shape=(
            jax.ShapeDtypeStruct((S_LOC, I_LOC, CM), F32),
            jax.ShapeDtypeStruct((I_LOC, J_LOC, CZ), F32),
        ),
        in_specs=[vm] * 9 + [sm] * 2,
        out_specs=(vm, vm),
        scratch_shapes=[
            pltpu.VMEM((2, I_LOC * HEADS, 128), F32),
            pltpu.VMEM((HEADS, I_LOC, 256), BF16),
            pltpu.VMEM((HEADS, I_LOC, 256), BF16),
            pltpu.VMEM((N_SEQ, 4, HEADS, I_LOC, 256), BF16),
            pltpu.VMEM((RES, RES), F32),
            pltpu.VMEM((RES, CM), F32),
            pltpu.VMEM((2, HEADS, 4, I_LOC, 128), F32),
            pltpu.VMEM((N_RES, 2, 3, I_LOC, 128), BF16),
            pltpu.VMEM((2, N_RES, 3, I_LOC, 128), BF16),
            pltpu.VMEM((RES, 128), BF16),
            pltpu.VMEM((RES, 128), BF16),
            pltpu.VMEM((RES, 128), BF16),
            pltpu.VMEM((2, RES, 128), F32),
            pltpu.VMEM((2, N_RES, I_LOC, 128), BF16),
            pltpu.VMEM((2, N_RES, I_LOC, 128), BF16),
            pltpu.VMEM((1024, 1024), BF16),
            pltpu.VMEM((S_LOC * I_LOC, 128), F32),
            pltpu.VMEM((I_LOC * OPM, 128), F32),
            pltpu.VMEM((S_LOC, I_LOC * OPM), BF16),
            pltpu.VMEM((I_LOC, OPM * S_LOC), BF16),
            pltpu.VMEM((N_SEQ, S_LOC, I_LOC * OPM), BF16),
            pltpu.VMEM((N_RES, I_LOC, OPM * S_LOC), BF16),
            pltpu.VMEM((I_LOC // 2, 512, 256), BF16),
            pltpu.VMEM((1024, 256), BF16),
            pltpu.VMEM((8 * JC, 512), BF16),
            pltpu.VMEM((I_LOC, JC, 1024), BF16),
            dma((2, N_RES)), dma((2, N_RES)),
            dma((8,)), dma((8,)), dma((8,)), dma((8,)), dma((2,)), dma((2,)),
            dma((2, N_RES)), dma((2, N_RES)),
            dma((4,)), dma((4,)), dma((N_RES,)), dma((N_RES,)),
            dma((4,)), dma((4,)),
        ],
        compiler_params=pltpu.CompilerParams(
            collective_id=0, has_side_effects=True, vmem_limit_bytes=VMEM_LIMIT
        ),
        name="evoformer",
    )(msa, pair, amino, poly, w, wshift.T, wmix, wfac.T, tmat, live, shifts)


def solution(mesh):
    in_specs = (P("seq", "res", None), P("res", "seq", None)) + (P(),) * 9
    out_specs = (P("seq", "res", None), P("res", "seq", None))
    return jax.shard_map(
        on_device, mesh=mesh, in_specs=in_specs, out_specs=out_specs, check_vma=False
    )
```

```python
import math

import jax
import jax.numpy as jnp
from jax import lax
from jax.experimental import pallas as pl
from jax.experimental.pallas import tpu as pltpu
from jax.sharding import PartitionSpec as P

MESH = pl.DeviceIdType.MESH
F32 = jnp.float32
BF16 = jnp.bfloat16
LOG2E = math.log2(math.e)
VMEM_LIMIT = 58 * 1024 * 1024

N_RES, N_SEQ = 32, 4
S_LOC, I_LOC, J_LOC = 32, 24, 192
CM, CZ, HEADS, HD, OPM = 256, 128, 8, 32, 32
RES = 768
Q_CHUNK = 256
J_BLOCKS = 2
JC = J_BLOCKS * I_LOC


def lane_iota(shape):
    return lax.broadcasted_iota(jnp.int32, shape, len(shape) - 1)


def in_slot(lane, k):
    return (lane >= k * 32) & (lane < (k + 1) * 32)


def layer_norm(x):
    centre = jnp.mean(x, axis=-1, keepdims=True)
    d = x - centre
    spread = jnp.mean(d * d, axis=-1, keepdims=True)
    return d * lax.rsqrt(spread + 1e-05)


def nt_dot(a, b, precision=None):
    return lax.dot_general(
        a, b, (((1,), (1,)), ((), ())), precision=precision, preferred_element_type=F32
    )


def offset(k, r):
    kk = lax.rem(k * 11, N_RES)
    x = lax.rem(lax.div(r, 8) + lax.div(kk, 8), 4)
    y = lax.rem(lax.div(r, 4) + lax.div(kk, 4), 2)
    z = lax.rem(r + kk, 4)
    return x * 8 + y * 4 + z


def exchange_lanes(tiles, width):
    lane = lane_iota(tiles[0].shape)
    tiles, bit = list(tiles), 1
    while bit < len(tiles):
        low = lax.rem(lane, 2 * bit * width) < bit * width
        new = list(tiles)
        for k in range(len(tiles)):
            if not k & bit:
                a, b = tiles[k], tiles[k | bit]
                new[k] = jnp.where(low, a, pltpu.roll(b, bit * width, 1))
                new[k | bit] = jnp.where(low, pltpu.roll(a, 128 - bit * width, 1), b)
        tiles, bit = new, 2 * bit
    return tiles


def remote(src, dst, a, b, d, q):
    return pltpu.make_async_remote_copy(
        src_ref=src, dst_ref=dst, send_sem=a, recv_sem=b, device_id=(d, q), device_id_type=MESH
    )


def kernel(
    msa, pair, amino, poly, w, wshift_t, wmix, wfac_t, tmat, live, shifts,
    family, contact,
    btmp, bsend, b1, br, bias, pgate, gate, qsend, recv, qs, ks, vs, acc, ret, back,
    bd_mix, fac, tr, lbuf, rbuf, lall, rall, lw, tcat, lhs, amat,
    ss, rs, s1, r1, s2, r2, s3, r3, sb, rb, sl, rl, sr, rr_sem, loc,
):
    r, s = lax.axis_index("res"), lax.axis_index("seq")
    h, z = lax.div(r, 4), lax.rem(r, 4)
    y_lo = lax.rem(h, 2)
    s_y = lax.rem(s + 2, 4)
    s_c = s + 1 - 2 * lax.rem(s, 2)
    b, mine = lax.div(r, 8), lax.rem(r, 8) * 4 + s
    holds = b == s

    def source(k):
        return 8 * s + lax.div(k, 4), lax.rem(k, 4)

    barrier = pltpu.get_barrier_semaphore()

    def greet(k, c):
        pl.semaphore_signal(barrier, inc=1, device_id=(offset(k, r), s), device_id_type=MESH)
        return c

    lax.fori_loop(1, N_RES, greet, 0)

    def greet_y(k, c):
        pl.semaphore_signal(barrier, inc=1, device_id=(h * 4 + k, s_y), device_id_type=MESH)
        return c

    lax.fori_loop(0, 4, greet_y, 0)

    def greet_seq(k, c):
        pl.semaphore_signal(barrier, inc=1, device_id=(r, lax.rem(s + k, 4)), device_id_type=MESH)
        return c

    lax.fori_loop(1, N_SEQ, greet_seq, 0)

    def greet_right(k, c):
        rr, q = source(k)

        @pl.when(jnp.logical_or(rr != r, q != s))
        def _():
            pl.semaphore_signal(barrier, inc=1, device_id=(rr, q), device_id_type=MESH)

        return c

    lax.fori_loop(0, N_RES, greet_right, 0)

    btmp[...] = jnp.zeros_like(btmp)
    chunk = 4
    for i0 in range(0, I_LOC, chunk):
        zn = layer_norm(pair[i0 : i0 + chunk].reshape(chunk * J_LOC, CZ))
        bb = nt_dot(wshift_t[...], zn, lax.Precision.HIGHEST)
        for i in range(chunk):
            rows, col = slice((i0 + i) * HEADS, (i0 + i + 1) * HEADS), i * J_LOC
            btmp[0, rows, :] = bb[:, col : col + 128]
            btmp[1, rows, 0:64] = bb[:, col + 128 : col + J_LOC]
    odd = jnp.full((I_LOC, 256), lax.rem(s, 2), jnp.int32) > 0
    for hh in range(HEADS):
        v = jnp.concatenate(
            [btmp[n, pl.ds(hh, I_LOC, stride=HEADS), :] for n in range(2)], axis=1
        )
        bsend[hh] = jnp.where(odd, pltpu.roll(v, 64, 1), v).astype(BF16)

    pl.semaphore_wait(barrier, 31 + 4 + 3 + N_RES - holds.astype(jnp.int32))

    pltpu.make_async_copy(bsend.at[h], b1.at[h], r1).start()

    def send1(k, c):
        hh = lax.rem(h + k, 8)
        remote(bsend.at[hh], b1.at[h], s1, r1, hh * 4 + z, s).start()
        return c

    lax.fori_loop(1, 8, send1, 0)

    normed = layer_norm(msa[...].reshape(S_LOC * I_LOC, CM)).astype(BF16)
    lane3 = lane_iota((8, I_LOC, 128))
    for part in range(3):
        out = jnp.dot(normed, w[:, part * CM : (part + 1) * CM], preferred_element_type=F32)
        if part == 0:
            out = out * F32(LOG2E / math.sqrt(HD))
        for t in range(2):
            cols = out[:, t * 128 : (t + 1) * 128].reshape(8, 4, I_LOC, 128)
            for a in range(4):
                tile = None
                for k in range(4):
                    piece = cols[:, k]
                    if (k - a) % 4:
                        piece = pltpu.roll(piece, (k - a) % 4 * 32, 2)
                    tile = piece if tile is None else jnp.where(in_slot(lane3, k), piece, tile)
                tile = tile.astype(BF16)
                for g in range(4):
                    for half in range(2):
                        qsend[(t * 4 + a) * 4 + g, half, part] = tile[g * 2 + half]

    def send_rows(half):
        pltpu.make_async_copy(qsend.at[r, half], recv.at[half, r], rs.at[half]).start()

        def send(k, c):
            d = offset(k, r)
            remote(qsend.at[d, half], recv.at[half, r], ss, rs.at[half], d, s).start()
            return c

        lax.fori_loop(1, N_RES, send, 0)

    send_rows(0)
    pltpu.make_async_copy(bsend, b1, r1).wait()
    slot = s * 4 + z
    own2 = pltpu.make_async_copy(b1, br.at[slot], loc.at[0])
    own2.start()

    def send2(k, c):
        zz = lax.rem(z + k, 4)
        q = lax.rem(s + 2 * lax.div(k, 4), 4)
        remote(b1, br.at[slot], s2, r2.at[lax.div(s, 2) * 4 + z], h * 4 + zz, q).start()
        return c

    lax.fori_loop(1, 8, send2, 0)
    remote(b1, br.at[slot], s3, r3, r, s_c).start()

    pgate[...] = jnp.dot(normed, w[:, 3 * CM :], preferred_element_type=F32).astype(BF16).astype(F32)
    for t in range(2):
        cols = jax.nn.sigmoid(pgate[:, t * 128 : (t + 1) * 128]).reshape(8, 4, I_LOC, 128)
        for a in range(4):
            tile = None
            for k in range(4):
                piece = cols[:, k]
                if (k - a) % 4:
                    piece = pltpu.roll(piece, (k - a) % 4 * 32, 2)
                tile = piece if tile is None else jnp.where(in_slot(lane3, k), piece, tile)
            for g in range(4):
                for half in range(2):
                    gate[half, t * 4 + a, g] = tile[g * 2 + half]
    bd_mix[...] = jnp.zeros_like(bd_mix)
    for hh in range(HEADS):
        for k in range(4):
            bd_mix[hh * 128 + k * 32 : hh * 128 + (k + 1) * 32, k * CM : (k + 1) * CM] = wmix[
                hh * HD : (hh + 1) * HD, :
            ]
    for e in range(OPM):
        t = tmat[pl.ds(e, OPM, stride=OPM), :]
        head = t.astype(BF16)
        tcat[e * 32 : (e + 1) * 32, 0:128] = head
        tcat[e * 32 : (e + 1) * 32, 128:256] = (t - head.astype(F32)).astype(BF16)
    acc[...] = jnp.zeros_like(acc)
    amino_row = amino[...].reshape(1, RES)
    poly_row = poly[...].reshape(1, RES)

    def column(row, n):
        tile = row[:, n * 128 : (n + 1) * 128].astype(F32)
        return jnp.transpose(jnp.broadcast_to(tile, (128, 128)), (1, 0))

    amino_col = [column(amino_row, n) for n in range(6)]
    for n in range(6):
        fac[n * 128 : (n + 1) * 128, :] = column(poly_row, n)

    remote(br.at[pl.ds(0, 7)], br.at[pl.ds(0, 7)], s2, r3, r, s_c).wait_send()
    send_rows(1)

    def wait2(k, c):
        zz = lax.rem(z + k, 4)
        q = lax.rem(s + 2 * lax.div(k, 4), 4)
        at = q * 4 + zz
        remote(b1, br.at[at], s2, r2.at[lax.div(q, 2) * 4 + zz], h * 4 + zz, q).wait_recv()
        remote(br.at[at], br.at[at], s3, r3, r, s_c).start()
        return c

    lax.fori_loop(1, 8, wait2, 0)
    own2.wait()
    remote(br.at[pl.ds(0, 8)], br.at[pl.ds(0, 8)], s3, r3, r, s_c).wait_recv()

    shift = shifts[h]
    lane24 = lane_iota((I_LOC, 128))
    poly_f = poly_row.astype(F32)

    def build(k, c):
        zz, hh = lax.rem(k, 4), lax.div(k, 4)
        row = pl.multiple_of(k * I_LOC, 8)
        own = fac[pl.ds(row, I_LOC), :]
        t = [br[q * 4 + zz, hh].astype(F32) for q in range(4)]
        tiles = [
            t[0][:, :128],
            jnp.where(lane24 < 64, t[0][:, 128:], t[1][:, :128]),
            t[1][:, 128:],
            t[2][:, :128],
            jnp.where(lane24 < 64, t[2][:, 128:], t[3][:, :128]),
            t[3][:, 128:],
        ]
        for n in range(6):
            cols = slice(n * 128, (n + 1) * 128)
            full = tiles[n] + jnp.where(own != poly_f[:, cols], shift, F32(0.0))
            full = jnp.where(amino_row[:, cols] > 0, full * F32(LOG2E), F32(-1e9))
            bias[pl.ds(row, I_LOC), cols] = full
        return c

    lax.fori_loop(0, N_RES, build, 0)

    lane_q = lane_iota((Q_CHUNK, 128))
    lane = lane_iota((RES, 128))
    for half in range(2):
        pltpu.make_async_copy(recv.at[half], recv.at[half], rs.at[half]).wait()
        qs[...] = recv[half, :, 0].astype(F32).reshape(RES, 128).astype(BF16)
        kf = recv[half, :, 1].astype(F32).reshape(RES, 128)
        for n in range(6):
            rows = slice(n * 128, (n + 1) * 128)
            ks[rows, :] = jnp.where(amino_col[n] > 0, kf[rows], F32(0.0)).astype(BF16)
        vs[...] = recv[half, :, 2].astype(F32).reshape(RES, 128).astype(BF16)

        def one_row(rr, c, half=half):
            slot = in_slot(lane, rr)
            xv = jnp.where(slot, vs[...].astype(F32), F32(1.0)).astype(BF16)
            xk = ks[...]
            slot_q = in_slot(lane_q, rr)
            for q0 in range(0, RES, Q_CHUNK):
                rows = slice(q0, q0 + Q_CHUNK)
                xq = jnp.where(slot_q, qs[rows, :].astype(F32), F32(0.0)).astype(BF16)
                sc = nt_dot(xq, xk) + bias[rows, :]
                m = jnp.max(sc, axis=-1, keepdims=True)
                p = jnp.exp2(sc - m).astype(BF16)
                o = jnp.dot(p, xv, preferred_element_type=F32)
                o = o / pltpu.roll(o, 32, 1)
                acc[half, rows, :] = jnp.where(slot_q, o, acc[half, rows, :])
            return c

        lax.fori_loop(0, 4, one_row, 0)
        ret[half] = acc[half].reshape(N_RES, I_LOC, 128).astype(BF16)
        pltpu.make_async_copy(ret.at[half, r], back.at[half, r], rb.at[half]).start()

        def send_back(k, c, half=half):
            d = offset(k, r)
            remote(ret.at[half, d], back.at[half, r], sb.at[half], rb.at[half], d, s).start()
            return c

        lax.fori_loop(1, N_RES, send_back, 0)

    def yz(k):
        kk = lax.rem(k * 3, 8)
        return lax.div(kk, 4), lax.rem(kk, 4)

    def send_left(half):
        pltpu.make_async_copy(lbuf.at[half], lall.at[s, half], rl).start()

        def send(k, c):
            q = lax.rem(s + k, 4)
            remote(lbuf.at[half], lall.at[s, half], sl, rl, r, q).start()
            return c

        lax.fori_loop(1, N_SEQ, send, 0)

    def send_right(half):
        blk = lax.rem(r, 8)

        @pl.when(holds)
        def _():
            pltpu.make_async_copy(rbuf.at[half], rall.at[blk, s, half], rr_sem.at[blk]).start()

        def send(k, c):
            dy, dz = yz(lax.div(k, 4))
            x = lax.rem(b + k, 4)
            d = x * 8 + lax.rem(y_lo + dy, 2) * 4 + lax.rem(z + dz, 4)

            @pl.when(jnp.logical_or(k != 0, jnp.logical_not(holds)))
            def _():
                remote(rbuf.at[half], rall.at[blk, s, half], sr, rr_sem.at[blk], d, b).start()

            return c

        lax.fori_loop(0, N_RES, send, 0)

    lane16 = lane_iota((16, 128))
    for n in range(6):
        tr[n * 128 : (n + 1) * 128, :] = amino_col[n]
    own_live = tr[pl.ds(pl.multiple_of(r * I_LOC, 8), I_LOC), :]
    for half in range(2):
        pltpu.make_async_copy(back.at[half], back.at[half], rb.at[half]).wait()
        gated = jnp.concatenate(
            [
                (back[half, 4 * hh : 4 * hh + 4].astype(F32) * gate[half, hh]).reshape(4 * I_LOC, 128)
                for hh in range(HEADS)
            ],
            axis=1,
        ).astype(BF16)
        for k in range(4):
            delta = jnp.dot(
                gated, bd_mix[:, k * CM : (k + 1) * CM], preferred_element_type=F32
            ).reshape(4, I_LOC, CM)
            fams = []
            for g in range(4):
                row = g * 8 + half * 4 + k
                fam = msa[row] + live[s * S_LOC + row].astype(F32) * delta[g]
                family[row] = fam
                fams.append(fam)
            y = layer_norm(jnp.concatenate(fams, axis=0)).astype(BF16)
            f = nt_dot(y, wfac_t[...])
            f = jnp.concatenate([f, jnp.zeros((4 * I_LOC, 64), F32)], axis=1)
            for g in range(4):
                on = live[s * S_LOC + g * 8 + half * 4 + k].astype(F32)
                at = (g * 4 + k) * I_LOC
                fac[at : at + I_LOC, :] = f[g * I_LOC : (g + 1) * I_LOC] * (on * own_live)
        for i0 in range(0, I_LOC, 4):
            tile = None
            for k in range(4):
                i = i0 + k
                f = fac[pl.ds(i, 16, stride=I_LOC), :]
                moved = pltpu.roll(f, k * 32, 1) if k else f
                tile = moved if tile is None else jnp.where(in_slot(lane16, k), moved, tile)
                ft = jnp.transpose(f, (1, 0))[OPM : 2 * OPM, :]
                tr[i * OPM : (i + 1) * OPM, :] = jnp.concatenate(
                    [ft, jnp.zeros((OPM, 112), F32)], axis=1
                )
            lbuf[half, :, i0 * 32 : (i0 + 4) * 32] = tile.astype(BF16)
        send_left(half)
        for e0 in range(0, OPM, 8):
            tile = tr[pl.ds(e0, I_LOC, stride=OPM), :]
            for k in range(1, 8):
                moved = pltpu.roll(tr[pl.ds(e0 + k, I_LOC, stride=OPM), :], k * 16, 1)
                tile = jnp.where(lane24 >= k * 16, moved, tile)
            rbuf[half, :, e0 * 16 : (e0 + 8) * 16] = tile.astype(BF16)
        send_right(half)

    pltpu.make_async_copy(lall, lall, rl).wait()
    left = lall[...].reshape(N_SEQ * S_LOC, I_LOC * OPM)
    for n in range(6):
        lw[n] = left[:, n * 128 : (n + 1) * 128]
    count = lax.fori_loop(0, 128, lambda k, c: c + live[k], jnp.int32(0)).astype(F32)
    inv = 1.0 / jnp.maximum(jnp.full((1, 128), count, F32), 1.0)

    for c0 in range(0, 8, J_BLOCKS):
        blocks = []
        for t in range(J_BLOCKS):
            dy, dz = yz(c0 + t)
            blocks.append(lax.rem(y_lo + 2 - dy, 2) * 4 + lax.rem(z + 4 - dz, 4))
        for blk in blocks:
            pltpu.make_async_copy(rall.at[blk], rall.at[blk], rr_sem.at[blk]).wait()
        for ge in range(4):
            cols = slice(ge * 128, (ge + 1) * 128)
            tiles = [
                jnp.concatenate([rall[blk, q, half, :, cols].astype(F32) for blk in blocks], axis=0)
                for q in range(N_SEQ)
                for half in range(2)
            ]
            for e, tile in enumerate(exchange_lanes(tiles, 16)):
                lhs[(ge * 8 + e) * JC : (ge * 8 + e + 1) * JC, :] = tile.astype(BF16)

        def spread(p, c):
            w2 = jnp.concatenate([lw[2 * p], lw[2 * p + 1]], axis=1)
            o = jnp.dot(lhs[...], w2, preferred_element_type=F32).astype(BF16)
            for t in range(2):
                for g in range(8):
                    tiles = [
                        o[(4 * g + k) * JC : (4 * g + k + 1) * JC, t * 128 : (t + 1) * 128]
                        for k in range(4)
                    ]
                    for m, tile in enumerate(exchange_lanes(tiles, 32)):
                        amat[(2 * p + t) * 4 + m, :, g * 128 : (g + 1) * 128] = tile
            return c

        lax.fori_loop(0, 3, spread, 0)

        def finish(p, c, blocks=tuple(blocks)):
            am = amat[pl.ds(12 * p, 12)].reshape(12 * JC, 1024)
            o = jnp.dot(am, tcat[...], preferred_element_type=F32)
            o = ((o[:, :128] + o[:, 128:]) * inv).reshape(12, JC, CZ)
            for t, blk in enumerate(blocks):
                at = (pl.ds(12 * p, 12), pl.ds(pl.multiple_of(blk * I_LOC, 8), I_LOC))
                contact[at] = pair[at] + o[:, t * I_LOC : (t + 1) * I_LOC]
            return c

        lax.fori_loop(0, I_LOC // 12, finish, 0)

    remote(bsend.at[pl.ds(0, 7)], b1.at[pl.ds(0, 7)], s1, r1, r, s_c).wait_send()
    remote(br.at[pl.ds(0, 8)], br.at[pl.ds(0, 8)], s3, r3, r, s_c).wait_send()
    remote(qsend.at[pl.ds(0, 31)], qsend.at[pl.ds(0, 31)], ss, r3, r, s_c).wait_send()
    for half in range(2):
        remote(
            ret.at[half, pl.ds(0, 31)], ret.at[half, pl.ds(0, 31)], sb.at[half], r3, r, s_c
        ).wait_send()
    remote(lall.at[pl.ds(0, 3)], lall.at[pl.ds(0, 3)], sl, r3, r, s_c).wait_send()
    remote(rall.at[pl.ds(0, 7)], rall.at[pl.ds(0, 7)], sr, r3, r, s_c).wait_send()
    last = rall.at[7, pl.ds(0, 3)]
    remote(last, last, sr, r3, r, s_c).wait_send()

    @pl.when(jnp.logical_not(holds))
    def _():
        rest = rall.at[7, 3]
        remote(rest, rest, sr, r3, r, s_c).wait_send()


def on_device(msa, pair, amino, poly, live, w, wshift, shifts, wmix, wfac, tmat):
    dma = pltpu.SemaphoreType.DMA
    vm = pl.BlockSpec(memory_space=pltpu.VMEM)
    sm = pl.BlockSpec(memory_space=pltpu.SMEM)
    return pl.pallas_call(
        kernel,
        out_shape=(
            jax.ShapeDtypeStruct((S_LOC, I_LOC, CM), F32),
            jax.ShapeDtypeStruct((I_LOC, J_LOC, CZ), F32),
        ),
        in_specs=[vm] * 9 + [sm] * 2,
        out_specs=(vm, vm),
        scratch_shapes=[
            pltpu.VMEM((2, I_LOC * HEADS, 128), F32),
            pltpu.VMEM((HEADS, I_LOC, 256), BF16),
            pltpu.VMEM((HEADS, I_LOC, 256), BF16),
            pltpu.VMEM((N_SEQ * 4, HEADS, I_LOC, 256), BF16),
            pltpu.VMEM((RES, RES), F32),
            pltpu.VMEM((RES, CM), F32),
            pltpu.VMEM((2, HEADS, 4, I_LOC, 128), F32),
            pltpu.VMEM((N_RES, 2, 3, I_LOC, 128), BF16),
            pltpu.VMEM((2, N_RES, 3, I_LOC, 128), BF16),
            pltpu.VMEM((RES, 128), BF16),
            pltpu.VMEM((RES, 128), BF16),
            pltpu.VMEM((RES, 128), BF16),
            pltpu.VMEM((2, RES, 128), F32),
            pltpu.VMEM((2, N_RES, I_LOC, 128), BF16),
            pltpu.VMEM((2, N_RES, I_LOC, 128), BF16),
            pltpu.VMEM((1024, 1024), BF16),
            pltpu.VMEM((S_LOC * I_LOC, 128), F32),
            pltpu.VMEM((I_LOC * OPM, 128), F32),
            pltpu.VMEM((2, 16, I_LOC * OPM), BF16),
            pltpu.VMEM((2, I_LOC, OPM * 16), BF16),
            pltpu.VMEM((N_SEQ, 2, 16, I_LOC * OPM), BF16),
            pltpu.VMEM((8, N_SEQ, 2, I_LOC, OPM * 16), BF16),
            pltpu.VMEM((6, N_SEQ * S_LOC, 128), BF16),
            pltpu.VMEM((1024, 256), BF16),
            pltpu.VMEM((OPM * JC, 128), BF16),
            pltpu.VMEM((I_LOC, JC, 1024), BF16),
            dma, dma((2,)), dma, dma, dma, dma((8,)), dma, dma,
            dma((2,)), dma((2,)), dma, dma, dma, dma((8,)), dma((1,)),
        ],
        compiler_params=pltpu.CompilerParams(
            collective_id=0, has_side_effects=True, vmem_limit_bytes=VMEM_LIMIT
        ),
        name="evoformer",
    )(msa, pair, amino, poly, w, wshift.T, wmix, wfac.T, tmat, live, shifts)


def solution(mesh):
    in_specs = (P("seq", "res", None), P("res", "seq", None)) + (P(),) * 9
    out_specs = (P("seq", "res", None), P("res", "seq", None))
    return jax.shard_map(
        on_device, mesh=mesh, in_specs=in_specs, out_specs=out_specs, check_vma=False
    )
```

```python
import math

import jax
import jax.numpy as jnp
from jax import lax
from jax.experimental import pallas as pl
from jax.experimental.pallas import tpu as pltpu
from jax.sharding import PartitionSpec as P

MESH = pl.DeviceIdType.MESH
F32 = jnp.float32
BF16 = jnp.bfloat16
LOG2E = math.log2(math.e)
VMEM_LIMIT = 58 * 1024 * 1024

N_RES, N_SEQ = 32, 4
S_LOC, I_LOC, J_LOC = 32, 24, 192
CM, CZ, HEADS, HD, OPM = 256, 128, 8, 32, 32
RES = 768
Q_CHUNK, K_CHUNK = 384, 256
OFFSETS = [((k * 11) % 32 // 8, (k * 11) % 8 // 4, (k * 11) % 4) for k in range(1, N_RES)]
YZ = [((k * 3) % 8 // 4, (k * 3) % 4) for k in range(8)]
J_BLOCKS = 2
JC = J_BLOCKS * I_LOC


def lane_iota(shape):
    return lax.broadcasted_iota(jnp.int32, shape, len(shape) - 1)


def in_slot(lane, k):
    return (lane >= k * 32) & (lane < (k + 1) * 32)


def layer_norm(x):
    centre = jnp.mean(x, axis=-1, keepdims=True)
    d = x - centre
    spread = jnp.mean(d * d, axis=-1, keepdims=True)
    return d * lax.rsqrt(spread + 1e-05)


def nt_dot(a, b, precision=None):
    return lax.dot_general(
        a, b, (((1,), (1,)), ((), ())), precision=precision, preferred_element_type=F32
    )


def exchange_lanes(tiles, width):
    lane = lane_iota(tiles[0].shape)
    tiles, bit = list(tiles), 1
    while bit < len(tiles):
        low = lax.rem(lane, 2 * bit * width) < bit * width
        new = list(tiles)
        for k in range(len(tiles)):
            if not k & bit:
                a, b = tiles[k], tiles[k | bit]
                new[k] = jnp.where(low, a, pltpu.roll(b, bit * width, 1))
                new[k | bit] = jnp.where(low, pltpu.roll(a, 128 - bit * width, 1), b)
        tiles, bit = new, 2 * bit
    return tiles


def remote(src, dst, a, b, d, q):
    return pltpu.make_async_remote_copy(
        src_ref=src, dst_ref=dst, send_sem=a, recv_sem=b, device_id=(d, q), device_id_type=MESH
    )


def kernel(
    msa_hbm, pair_hbm, w_hbm, wmix_hbm, tmat_hbm, amino, poly, wshift_t, wfac_t, live, shifts,
    delta_hbm, proj_hbm,
    msa, pair, w, wmix, tmat, dbuf, pbuf,
    btmp, bsend, b1, b2, br, bias, pgate, gate, qsend, recv, qs, ks, vs, acc, ret, back,
    wrep, wfac, fac, tr, lbuf, rbuf, lall, rall, lw, tcat, lhs, amat,
    ss, rs, s1, r1, s2, r2, s3, r3, sb, rb, sl, rl, sr, rr_sem, loc, ins, outs,
):
    r, s = lax.axis_index("res"), lax.axis_index("seq")
    h, z = lax.div(r, 4), lax.rem(r, 4)
    y_lo, b = lax.rem(h, 2), lax.div(r, 8)
    s_c = s + 1 - 2 * lax.rem(s, 2)
    holds = b == s
    xs = [lax.rem(b + k, 4) * 8 for k in range(4)]
    ys = [lax.rem(y_lo + k, 2) * 4 for k in range(2)]
    zs = [lax.rem(z + k, 4) for k in range(4)]
    seqs = [lax.rem(s + k, 4) for k in range(4)]
    partners = [xs[i] + ys[j] + zs[k] for i, j, k in OFFSETS]

    loads = [
        pltpu.make_async_copy(src, dst, ins.at[6 + n])
        for n, (src, dst) in enumerate(
            ((msa_hbm, msa), (w_hbm, w), (wmix_hbm, wmix), (tmat_hbm, tmat))
        )
    ]
    pair_loads = [
        pltpu.make_async_copy(pair_hbm.at[pl.ds(4 * n, 4)], pair.at[pl.ds(4 * n, 4)], ins.at[n])
        for n in range(6)
    ]
    for cp in loads[:2] + pair_loads + loads[2:]:
        cp.start()

    barrier = pltpu.get_barrier_semaphore()

    def greet(d, q):
        pl.semaphore_signal(barrier, inc=1, device_id=(d, q), device_id_type=MESH)

    for d in partners:
        greet(d, s)
    for k in range(4):
        greet(h * 4 + k, seqs[2])
    for k in range(1, N_SEQ):
        greet(r, seqs[k])
    for dy, dz in YZ:
        for k in range(N_SEQ):
            if dy or dz or k:
                greet(8 * s + ys[dy] + zs[dz], seqs[k])

    @pl.when(jnp.logical_not(holds))
    def _():
        greet(8 * s + ys[0] + zs[0], s)

    loads[0].wait()
    loads[1].wait()
    normed = layer_norm(msa[...].reshape(S_LOC * I_LOC, CM)).astype(BF16)
    lane3 = lane_iota((8, I_LOC, 128))
    for part in range(3):
        out = jnp.dot(normed, w[:, part * CM : (part + 1) * CM], preferred_element_type=F32)
        if part == 0:
            out = out * F32(LOG2E / math.sqrt(HD))
        for t in range(2):
            cols = out[:, t * 128 : (t + 1) * 128].reshape(8, 4, I_LOC, 128)
            for a in range(4):
                tile = None
                for k in range(4):
                    piece = cols[:, k]
                    if (k - a) % 4:
                        piece = pltpu.roll(piece, (k - a) % 4 * 32, 2)
                    tile = piece if tile is None else jnp.where(in_slot(lane3, k), piece, tile)
                tile = tile.astype(BF16)
                for g in range(4):
                    for half in range(2):
                        qsend[(t * 4 + a) * 4 + g, half, part] = tile[g * 2 + half]

    btmp[...] = jnp.zeros_like(btmp)
    chunk = 4
    for i0 in range(0, I_LOC, chunk):
        pair_loads[i0 // chunk].wait()
        zn = layer_norm(pair[i0 : i0 + chunk].reshape(chunk * J_LOC, CZ))
        bb = nt_dot(wshift_t[...], zn, lax.Precision.HIGHEST)
        for i in range(chunk):
            rows, col = slice((i0 + i) * HEADS, (i0 + i + 1) * HEADS), i * J_LOC
            btmp[0, rows, :] = bb[:, col : col + 128]
            btmp[1, rows, 0:64] = bb[:, col + 128 : col + J_LOC]
    odd = jnp.full((I_LOC, 128), lax.rem(s, 2), jnp.int32) > 0
    swap = jnp.full((I_LOC, 128), lax.rem(h, 2), jnp.int32) > 0
    lane24 = lane_iota((I_LOC, 128))
    low24 = lane24 < 64
    for hh in range(HEADS):
        v0, v1 = (btmp[n, pl.ds(hh, I_LOC, stride=HEADS), :] for n in range(2))
        t0, t1 = pltpu.roll(v0, 64, 1), pltpu.roll(v1, 64, 1)
        bsend[hh, 0] = jnp.where(odd, jnp.where(low24, t0, t1), v0).astype(BF16)
        part = jnp.where(odd, v0, v1)
        bsend[hh, 1] = jnp.where(swap, pltpu.roll(part, 64, 1), part).astype(BF16)

    pl.semaphore_wait(barrier, 31 + 4 + 3 + N_RES - holds.astype(jnp.int32))

    def send_rows(half):
        pltpu.make_async_copy(qsend.at[r, half], recv.at[half, r], rs.at[half]).start()
        for d in partners:
            remote(qsend.at[d, half], recv.at[half, r], ss, rs.at[half], d, s).start()

    pltpu.make_async_copy(bsend.at[h], b1.at[h], r1).start()
    for i in range(4):
        for j in range(2):
            if i or j:
                d = xs[i] + ys[j] + z
                remote(bsend.at[lax.div(d, 4)], b1.at[h], s1, r1, d, s).start()

    send_rows(0)

    pgate[...] = jnp.dot(normed, w[:, 3 * CM :], preferred_element_type=F32).astype(BF16).astype(F32)
    for t in range(2):
        cols = jax.nn.sigmoid(pgate[:, t * 128 : (t + 1) * 128]).reshape(8, 4, I_LOC, 128)
        for a in range(4):
            tile = None
            for k in range(4):
                piece = cols[:, k]
                if (k - a) % 4:
                    piece = pltpu.roll(piece, (k - a) % 4 * 32, 2)
                tile = piece if tile is None else jnp.where(in_slot(lane3, k), piece, tile)
            for g in range(4):
                for half in range(2):
                    gate[half, t * 4 + a, g] = tile[g * 2 + half]

    pltpu.make_async_copy(bsend, b1, r1).wait()
    for k in range(HEADS):
        b2[k] = b1[k, 0]
    for k in range(4):
        b2[8 + k] = jnp.where(
            low24, b1[2 * k, 1].astype(F32), b1[2 * k + 1, 1].astype(F32)
        ).astype(BF16)
    slot = s * 4 + z
    mine2 = lax.div(s, 2) * 4 + z
    own2 = pltpu.make_async_copy(b2, br.at[slot], loc.at[0])
    own2.start()
    for k in range(1, 8):
        zz, q = zs[k // 2], seqs[k % 2 * 2]
        remote(b2, br.at[slot], s2, r2.at[mine2], h * 4 + zz, q).start()
    remote(b2, br.at[slot], s3, r3.at[z], r, s_c).start()

    loads[2].wait()
    loads[3].wait()
    for hh in range(HEADS):
        for k in range(4):
            wrep[hh * 128 + k * 32 : hh * 128 + (k + 1) * 32, :] = wmix[hh * HD : (hh + 1) * HD, :]
    wfac[...] = jnp.concatenate([wfac_t[...], jnp.zeros((64, CM), BF16)], axis=0)
    for e in range(OPM):
        t = tmat[pl.ds(e, OPM, stride=OPM), :]
        head = t.astype(BF16)
        tcat[e * 32 : (e + 1) * 32, 0:128] = head
        tcat[e * 32 : (e + 1) * 32, 128:256] = (t - head.astype(F32)).astype(BF16)
    acc[...] = jnp.zeros_like(acc)
    amino_row = amino[...].reshape(1, RES)
    poly_row = poly[...].reshape(1, RES)

    def column(row, n):
        tile = row[:, n * 128 : (n + 1) * 128].astype(F32)
        return jnp.transpose(jnp.broadcast_to(tile, (128, 128)), (1, 0))

    amino_col = [column(amino_row, n) for n in range(6)]
    for n in range(6):
        fac[n * 128 : (n + 1) * 128, :] = column(poly_row, n)

    remote(br.at[pl.ds(0, 7)], br.at[pl.ds(0, 7)], s2, r1, r, s_c).wait_send()
    send_rows(1)

    shift = shifts[h]
    poly_f = poly_row.astype(F32)

    def build(zz, pair_n):
        for parity in range(2):
            hh = 2 * pair_n + parity
            row = pl.multiple_of((hh * 4 + zz) * I_LOC, 8)
            own = fac[pl.ds(row, I_LOC), :]
            full = [br[q * 4 + zz, hh].astype(F32) for q in range(4)]
            part = [br[q * 4 + zz, 8 + pair_n].astype(F32) for q in range(4)]
            for q in range(4):
                if q % 2 != parity:
                    part[q] = pltpu.roll(part[q], 64, 1)
            tiles = [
                full[0], jnp.where(low24, part[0], part[1]), full[1],
                full[2], jnp.where(low24, part[2], part[3]), full[3],
            ]
            for n in range(6):
                cols = slice(n * 128, (n + 1) * 128)
                val = tiles[n] + jnp.where(own != poly_f[:, cols], shift, F32(0.0))
                val = jnp.where(amino_row[:, cols] > 0, val * F32(LOG2E), F32(-1e9))
                bias[pl.ds(row, I_LOC), cols] = val

    def finish_z(zz):
        remote(br.at[pl.ds(0, 2)], br.at[pl.ds(0, 2)], s3, r3.at[zz], r, s_c).wait_recv()

        def step(pair_n, c):
            build(zz, pair_n)
            return c

        lax.fori_loop(0, 4, step, 0)

    own2.wait()
    before = None
    for k in (0, 3, 2, 1):
        for y in range(2):
            if k or y:
                zz, q = zs[k], seqs[2 * y]
                at = q * 4 + zz
                remote(
                    b2, br.at[at], s2, r2.at[lax.div(q, 2) * 4 + zz], h * 4 + zz, q
                ).wait_recv()
                remote(br.at[at], br.at[at], s3, r3.at[zz], r, s_c).start()
        if before is not None:
            finish_z(before)
        before = zs[k]
    finish_z(before)

    lane_q = lane_iota((Q_CHUNK, 128))
    lane = lane_iota((RES, 128))
    for half in range(2):
        pltpu.make_async_copy(recv.at[half], recv.at[half], rs.at[half]).wait()
        qs[...] = recv[half, :, 0].astype(F32).reshape(RES, 128).astype(BF16)
        kf = recv[half, :, 1].astype(F32).reshape(RES, 128)
        for n in range(6):
            rows = slice(n * 128, (n + 1) * 128)
            ks[rows, :] = jnp.where(amino_col[n] > 0, kf[rows], F32(0.0)).astype(BF16)
        vs[...] = recv[half, :, 2].astype(F32).reshape(RES, 128).astype(BF16)

        def one_row(rr):
            slot = in_slot(lane, rr)
            xv = jnp.where(slot, vs[...].astype(F32), F32(1.0)).astype(BF16)
            xk = ks[...]
            slot_q = in_slot(lane_q, rr)
            for q0 in range(0, RES, Q_CHUNK):
                rows = slice(q0, q0 + Q_CHUNK)
                xq = jnp.where(slot_q, qs[rows, :].astype(F32), F32(0.0)).astype(BF16)
                o = m = None
                for k0 in range(0, RES, K_CHUNK):
                    keys = slice(k0, k0 + K_CHUNK)
                    sc = nt_dot(xq, xk[keys]) + bias[rows, keys]
                    m1 = jnp.max(sc, axis=-1, keepdims=True)
                    p = jnp.exp2(sc - m1).astype(BF16)
                    o1 = jnp.dot(p, xv[keys], preferred_element_type=F32)
                    if o is None:
                        o, m = o1, m1
                    else:
                        top = jnp.maximum(m, m1)
                        o = o * jnp.exp2(m - top) + o1 * jnp.exp2(m1 - top)
                        m = top
                o = o / pltpu.roll(o, 32, 1)
                acc[half, rows, :] = jnp.where(slot_q, o, acc[half, rows, :])

        def two_rows(rr, c):
            one_row(2 * rr)
            one_row(2 * rr + 1)
            return c

        lax.fori_loop(0, 2, two_rows, 0)
        ret[half] = acc[half].reshape(N_RES, I_LOC, 128).astype(BF16)
        pltpu.make_async_copy(ret.at[half, r], back.at[half, r], rb.at[half]).start()

        for d in partners:
            remote(ret.at[half, d], back.at[half, r], sb.at[half], rb.at[half], d, s).start()

    def send_left(half):
        pltpu.make_async_copy(lbuf.at[half], lall.at[s, half], rl).start()
        for k in range(1, N_SEQ):
            remote(lbuf.at[half], lall.at[s, half], sl, rl, r, seqs[k]).start()

    blk_r = lax.rem(r, 8)

    def send_right(half, k):
        dy, dz = YZ[k // 4]
        cp = remote(
            rbuf.at[half], rall.at[blk_r, s, half], sr, rr_sem.at[blk_r], xs[k % 4] + ys[dy] + zs[dz], b
        )
        if k:
            cp.start()
        else:

            @pl.when(holds)
            def _():
                pltpu.make_async_copy(rbuf.at[half], rall.at[blk_r, s, half], rr_sem.at[blk_r]).start()

            @pl.when(jnp.logical_not(holds))
            def _():
                cp.start()

    lane16 = lane_iota((16, 128))
    lane96 = lane_iota((4 * I_LOC, 128))
    for n in range(6):
        tr[n * 128 : (n + 1) * 128, :] = amino_col[n]
    own_live = tr[pl.ds(pl.multiple_of(r * I_LOC, 8), I_LOC), :]
    for half in range(2):
        pltpu.make_async_copy(back.at[half], back.at[half], rb.at[half]).wait()
        heads = [
            (back[half, 4 * hh : 4 * hh + 4].astype(F32) * gate[half, hh]).reshape(4 * I_LOC, 128)
            for hh in range(HEADS)
        ]
        gated = jnp.concatenate(
            [
                jnp.concatenate(
                    [jnp.where(in_slot(lane96, k), t, F32(0.0)).astype(BF16) for t in heads], axis=1
                )
                for k in range(4)
            ],
            axis=0,
        )
        delta = jnp.dot(gated, wrep[...], preferred_element_type=F32).reshape(16, I_LOC, CM)
        fams = []
        for k in range(4):
            for g in range(4):
                row = g * 8 + half * 4 + k
                step = live[s * S_LOC + row].astype(F32) * delta[k * 4 + g]
                dbuf[row] = step
                fams.append(msa[row] + step)
        y = layer_norm(jnp.concatenate(fams, axis=0)).astype(BF16)
        f = nt_dot(y, wfac[...])
        for k in range(4):
            for g in range(4):
                on = live[s * S_LOC + g * 8 + half * 4 + k].astype(F32)
                at = (k * 4 + g) * I_LOC
                fac[at : at + I_LOC, :] = f[at : at + I_LOC] * (on * own_live)
        for i0 in range(0, I_LOC, 4):
            tile = None
            for k in range(4):
                i = i0 + k
                f = fac[pl.ds(i, 16, stride=I_LOC), :]
                moved = pltpu.roll(f, k * 32, 1) if k else f
                tile = moved if tile is None else jnp.where(in_slot(lane16, k), moved, tile)
                ft = jnp.transpose(f, (1, 0))[OPM : 2 * OPM, :]
                tr[i * OPM : (i + 1) * OPM, :] = jnp.concatenate(
                    [ft, jnp.zeros((OPM, 112), F32)], axis=1
                )
            lbuf[half, :, i0 * 32 : (i0 + 4) * 32] = tile.astype(BF16)
        send_left(half)
        for e0 in range(0, OPM, 8):
            tile = tr[pl.ds(e0, I_LOC, stride=OPM), :]
            for k in range(1, 8):
                moved = pltpu.roll(tr[pl.ds(e0 + k, I_LOC, stride=OPM), :], k * 16, 1)
                tile = jnp.where(lane24 >= k * 16, moved, tile)
            rbuf[half, :, e0 * 16 : (e0 + 8) * 16] = tile.astype(BF16)
        if half == 0:
            for k in range(16):
                send_right(0, k)
        else:
            for k in range(16):
                send_right(1, k)
            for k in range(16, N_RES):
                send_right(0, k)
                send_right(1, k)
            out_delta = pltpu.make_async_copy(dbuf, delta_hbm, outs.at[16])
            out_delta.start()

    def take_left():
        pltpu.make_async_copy(lall, lall, rl).wait()
        left = lall[...].reshape(N_SEQ * S_LOC, I_LOC * OPM)
        for n in range(6):
            lw[n] = left[:, n * 128 : (n + 1) * 128]

    count = lax.fori_loop(0, 128, lambda k, c: c + live[k], jnp.int32(0)).astype(F32)
    inv = 1.0 / jnp.maximum(jnp.full((1, 128), count, F32), 1.0)

    out_proj = []
    for c0 in range(0, 8, J_BLOCKS):
        blocks = []
        for t in range(J_BLOCKS):
            dy, dz = YZ[c0 + t]
            blocks.append(ys[dy] + zs[(4 - dz) % 4])
        for blk in blocks:
            pltpu.make_async_copy(rall.at[blk], rall.at[blk], rr_sem.at[blk]).wait()
        for ge in range(4):
            cols = slice(ge * 128, (ge + 1) * 128)
            tiles = [
                jnp.concatenate([rall[blk, q, half, :, cols].astype(F32) for blk in blocks], axis=0)
                for q in range(N_SEQ)
                for half in range(2)
            ]
            for e, tile in enumerate(exchange_lanes(tiles, 16)):
                lhs[(ge * 8 + e) * JC : (ge * 8 + e + 1) * JC, :] = tile.astype(BF16)
        if c0 == 0:
            take_left()

        def spread(p, c):
            w2 = jnp.concatenate([lw[2 * p], lw[2 * p + 1]], axis=1)
            o = jnp.dot(lhs[...], w2, preferred_element_type=F32).astype(BF16)
            for t in range(2):
                for g in range(8):
                    tiles = [
                        o[(4 * g + k) * JC : (4 * g + k + 1) * JC, t * 128 : (t + 1) * 128]
                        for k in range(4)
                    ]
                    for m, tile in enumerate(exchange_lanes(tiles, 32)):
                        amat[(2 * p + t) * 4 + m, :, g * 128 : (g + 1) * 128] = tile
            return c

        lax.fori_loop(0, 3, spread, 0)

        for p in range(2):
            some = pl.ds(12 * p, 12)
            o = jnp.dot(amat[some].reshape(12 * JC, 1024), tcat[...], preferred_element_type=F32)
            o = ((o[:, :128] + o[:, 128:]) * inv).reshape(12, JC, CZ)
            for t, blk in enumerate(blocks):
                pbuf[blk, some] = o[:, t * I_LOC : (t + 1) * I_LOC]
                out = pltpu.make_async_copy(
                    pbuf.at[blk, some],
                    proj_hbm.at[some, pl.ds(pl.multiple_of(blk * I_LOC, 8), I_LOC)],
                    outs.at[2 * (c0 + t) + p],
                )
                out.start()
                out_proj.append(out)

    out_delta.wait()
    for out in out_proj:
        out.wait()
    remote(bsend.at[pl.ds(0, 7)], b1.at[pl.ds(0, 7)], s1, r1, r, s_c).wait_send()
    remote(br.at[pl.ds(0, 8)], br.at[pl.ds(0, 8)], s3, r1, r, s_c).wait_send()
    remote(qsend.at[pl.ds(0, 31)], qsend.at[pl.ds(0, 31)], ss, r1, r, s_c).wait_send()
    for half in range(2):
        remote(
            ret.at[half, pl.ds(0, 31)], ret.at[half, pl.ds(0, 31)], sb.at[half], r1, r, s_c
        ).wait_send()
    remote(lall.at[pl.ds(0, 3)], lall.at[pl.ds(0, 3)], sl, r1, r, s_c).wait_send()
    remote(rall.at[pl.ds(0, 7)], rall.at[pl.ds(0, 7)], sr, r1, r, s_c).wait_send()
    last = rall.at[7, pl.ds(0, 3)]
    remote(last, last, sr, r1, r, s_c).wait_send()

    @pl.when(jnp.logical_not(holds))
    def _():
        rest = rall.at[7, 3]
        remote(rest, rest, sr, r1, r, s_c).wait_send()


def on_device(msa, pair, amino, poly, live, w, wshift, shifts, wmix, wfac, tmat):
    dma = pltpu.SemaphoreType.DMA
    vm = pl.BlockSpec(memory_space=pltpu.VMEM)
    sm = pl.BlockSpec(memory_space=pltpu.SMEM)
    hbm = pl.BlockSpec(memory_space=pl.ANY)
    delta, proj = pl.pallas_call(
        kernel,
        out_shape=(
            jax.ShapeDtypeStruct((S_LOC, I_LOC, CM), F32),
            jax.ShapeDtypeStruct((I_LOC, J_LOC, CZ), F32),
        ),
        in_specs=[hbm] * 5 + [vm] * 4 + [sm] * 2,
        out_specs=(hbm, hbm),
        scratch_shapes=[
            pltpu.VMEM((S_LOC, I_LOC, CM), F32),
            pltpu.VMEM((I_LOC, J_LOC, CZ), F32),
            pltpu.VMEM((CM, 4 * CM), BF16),
            pltpu.VMEM((CM, CM), BF16),
            pltpu.VMEM((OPM * OPM, CZ), F32),
            pltpu.VMEM((S_LOC, I_LOC, CM), F32),
            pltpu.VMEM((8, I_LOC, I_LOC, CZ), F32),
            pltpu.VMEM((2, I_LOC * HEADS, 128), F32),
            pltpu.VMEM((HEADS, 2, I_LOC, 128), BF16),
            pltpu.VMEM((HEADS, 2, I_LOC, 128), BF16),
            pltpu.VMEM((12, I_LOC, 128), BF16),
            pltpu.VMEM((N_SEQ * 4, 12, I_LOC, 128), BF16),
            pltpu.VMEM((RES, RES), F32),
            pltpu.VMEM((RES, CM), F32),
            pltpu.VMEM((2, HEADS, 4, I_LOC, 128), F32),
            pltpu.VMEM((N_RES, 2, 3, I_LOC, 128), BF16),
            pltpu.VMEM((2, N_RES, 3, I_LOC, 128), BF16),
            pltpu.VMEM((RES, 128), BF16),
            pltpu.VMEM((RES, 128), BF16),
            pltpu.VMEM((RES, 128), BF16),
            pltpu.VMEM((2, RES, 128), F32),
            pltpu.VMEM((2, N_RES, I_LOC, 128), BF16),
            pltpu.VMEM((2, N_RES, I_LOC, 128), BF16),
            pltpu.VMEM((1024, CM), BF16),
            pltpu.VMEM((128, CM), BF16),
            pltpu.VMEM((RES, 128), F32),
            pltpu.VMEM((I_LOC * OPM, 128), F32),
            pltpu.VMEM((2, 16, I_LOC * OPM), BF16),
            pltpu.VMEM((2, I_LOC, OPM * 16), BF16),
            pltpu.VMEM((N_SEQ, 2, 16, I_LOC * OPM), BF16),
            pltpu.VMEM((8, N_SEQ, 2, I_LOC, OPM * 16), BF16),
            pltpu.VMEM((6, N_SEQ * S_LOC, 128), BF16),
            pltpu.VMEM((1024, 256), BF16),
            pltpu.VMEM((OPM * JC, 128), BF16),
            pltpu.VMEM((I_LOC, JC, 1024), BF16),
            dma, dma((2,)), dma, dma, dma, dma((8,)), dma, dma((4,)),
            dma((2,)), dma((2,)), dma, dma, dma, dma((8,)), dma((1,)),
            dma((10,)), dma((17,)),
        ],
        compiler_params=pltpu.CompilerParams(
            collective_id=0, has_side_effects=True, vmem_limit_bytes=VMEM_LIMIT
        ),
        name="evoformer",
    )(msa, pair, w, wmix, tmat, amino, poly, wshift.T, wfac.T, live, shifts)
    return msa + delta, pair + proj


def solution(mesh):
    in_specs = (P("seq", "res", None), P("res", "seq", None)) + (P(),) * 9
    out_specs = (P("seq", "res", None), P("res", "seq", None))
    return jax.shard_map(
        on_device, mesh=mesh, in_specs=in_specs, out_specs=out_specs, check_vma=False
    )
```

```python
import math

import jax
import jax.numpy as jnp
from jax import lax
from jax.experimental import pallas as pl
from jax.experimental.pallas import tpu as pltpu
from jax.sharding import PartitionSpec as P

MESH = pl.DeviceIdType.MESH
F32 = jnp.float32
BF16 = jnp.bfloat16
LOG2E = math.log2(math.e)
VMEM_LIMIT = 58 * 1024 * 1024

N_RES, N_SEQ = 32, 4
S_LOC, I_LOC, J_LOC = 32, 24, 192
CM, CZ, HEADS, HD, OPM = 256, 128, 8, 32, 32
RES = 768
Q_CHUNK, K_CHUNK = 384, 256
OFFSETS = [((k * 11) % 32 // 8, (k * 11) % 8 // 4, (k * 11) % 4) for k in range(1, N_RES)]
YZ = [((k * 3) % 8 // 4, (k * 3) % 4) for k in range(8)]
J_BLOCKS = 2
JC = J_BLOCKS * I_LOC


def lane_iota(shape):
    return lax.broadcasted_iota(jnp.int32, shape, len(shape) - 1)


def in_slot(lane, k):
    return (lane >= k * 32) & (lane < (k + 1) * 32)


def layer_norm(x):
    centre = jnp.mean(x, axis=-1, keepdims=True)
    d = x - centre
    spread = jnp.mean(d * d, axis=-1, keepdims=True)
    return d * lax.rsqrt(spread + 1e-05)


def nt_dot(a, b, precision=None):
    return lax.dot_general(
        a, b, (((1,), (1,)), ((), ())), precision=precision, preferred_element_type=F32
    )


def exchange_lanes(tiles, width):
    lane = lane_iota(tiles[0].shape)
    tiles, bit = list(tiles), 1
    while bit < len(tiles):
        low = lax.rem(lane, 2 * bit * width) < bit * width
        new = list(tiles)
        for k in range(len(tiles)):
            if not k & bit:
                a, b = tiles[k], tiles[k | bit]
                new[k] = jnp.where(low, a, pltpu.roll(b, bit * width, 1))
                new[k | bit] = jnp.where(low, pltpu.roll(a, 128 - bit * width, 1), b)
        tiles, bit = new, 2 * bit
    return tiles


def remote(src, dst, a, b, d, q):
    return pltpu.make_async_remote_copy(
        src_ref=src, dst_ref=dst, send_sem=a, recv_sem=b, device_id=(d, q), device_id_type=MESH
    )


def kernel(
    msa_hbm, pair_hbm, w_hbm, wmix_hbm, tmat_hbm, amino, poly, wshift_t, wfac_t, live, shifts,
    delta_hbm, proj_hbm,
    msa, pair, w, wmix, tmat, dbuf, pbuf,
    btmp, bsend, b1, b2, br, bias, pgate, gate, qsend, recv, qs, ks, vs, acc, ret, back,
    wrep, wfac, fac, tr, lbuf, xbuf, lall, rall, lw, tcat, lhs, amat,
    ss, rs, s1, r1, s2, r2, s3, r3, sb, rb, sl, rl, sx, rx, sr, rr_sem, loc, ins, outs,
):
    r, s = lax.axis_index("res"), lax.axis_index("seq")
    h, z = lax.div(r, 4), lax.rem(r, 4)
    y_lo, b = lax.rem(h, 2), lax.div(r, 8)
    s_c = s + 1 - 2 * lax.rem(s, 2)
    xs = [lax.rem(b + k, 4) * 8 for k in range(4)]
    ys = [lax.rem(y_lo + k, 2) * 4 for k in range(2)]
    zs = [lax.rem(z + k, 4) for k in range(4)]
    seqs = [lax.rem(s + k, 4) for k in range(4)]
    partners = [xs[i] + ys[j] + zs[k] for i, j, k in OFFSETS]

    loads = [
        pltpu.make_async_copy(src, dst, ins.at[6 + n])
        for n, (src, dst) in enumerate(
            ((msa_hbm, msa), (w_hbm, w), (wmix_hbm, wmix), (tmat_hbm, tmat))
        )
    ]
    pair_loads = [
        pltpu.make_async_copy(pair_hbm.at[pl.ds(4 * n, 4)], pair.at[pl.ds(4 * n, 4)], ins.at[n])
        for n in range(6)
    ]
    for cp in loads[:2] + pair_loads + loads[2:]:
        cp.start()

    barrier = pltpu.get_barrier_semaphore()

    def greet(d, q):
        pl.semaphore_signal(barrier, inc=1, device_id=(d, q), device_id_type=MESH)

    for d in partners:
        greet(d, s)
    for k in range(4):
        greet(h * 4 + k, seqs[2])
    for k in range(1, N_SEQ):
        greet(r, seqs[k])
    for dy, dz in YZ:
        for k in range(N_SEQ):
            if dy or dz or k:
                greet(8 * b + ys[dy] + zs[dz], seqs[k])

    loads[0].wait()
    loads[1].wait()
    normed = layer_norm(msa[...].reshape(S_LOC * I_LOC, CM)).astype(BF16)
    lane3 = lane_iota((8, I_LOC, 128))
    for part in range(3):
        out = jnp.dot(normed, w[:, part * CM : (part + 1) * CM], preferred_element_type=F32)
        if part == 0:
            out = out * F32(LOG2E / math.sqrt(HD))
        for t in range(2):
            cols = out[:, t * 128 : (t + 1) * 128].reshape(8, 4, I_LOC, 128)
            for a in range(4):
                tile = None
                for k in range(4):
                    piece = cols[:, k]
                    if (k - a) % 4:
                        piece = pltpu.roll(piece, (k - a) % 4 * 32, 2)
                    tile = piece if tile is None else jnp.where(in_slot(lane3, k), piece, tile)
                tile = tile.astype(BF16)
                for g in range(4):
                    for half in range(2):
                        qsend[(t * 4 + a) * 4 + g, half, part] = tile[g * 2 + half]

    btmp[...] = jnp.zeros_like(btmp)
    chunk = 4
    for cp in pair_loads:
        cp.wait()
    for i0 in range(0, I_LOC, chunk):
        zn = layer_norm(pair[i0 : i0 + chunk].reshape(chunk * J_LOC, CZ))
        bb = nt_dot(wshift_t[...], zn, lax.Precision.HIGHEST)
        for i in range(chunk):
            rows, col = slice((i0 + i) * HEADS, (i0 + i + 1) * HEADS), i * J_LOC
            btmp[0, rows, :] = bb[:, col : col + 128]
            btmp[1, rows, 0:64] = bb[:, col + 128 : col + J_LOC]
    odd = jnp.full((I_LOC, 128), lax.rem(s, 2), jnp.int32) > 0
    swap = jnp.full((I_LOC, 128), lax.rem(h, 2), jnp.int32) > 0
    lane24 = lane_iota((I_LOC, 128))
    low24 = lane24 < 64
    for hh in range(HEADS):
        v0, v1 = (btmp[n, pl.ds(hh, I_LOC, stride=HEADS), :] for n in range(2))
        t0, t1 = pltpu.roll(v0, 64, 1), pltpu.roll(v1, 64, 1)
        bsend[hh, 0] = jnp.where(odd, jnp.where(low24, t0, t1), v0).astype(BF16)
        part = jnp.where(odd, v0, v1)
        bsend[hh, 1] = jnp.where(swap, pltpu.roll(part, 64, 1), part).astype(BF16)

    pl.semaphore_wait(barrier, 31 + 4 + 3 + 31)

    def send_rows(half, some):
        for d in some:
            remote(qsend.at[d, half], recv.at[half, r], ss, rs.at[half], d, s).start()

    for half in range(2):
        pltpu.make_async_copy(qsend.at[r, half], recv.at[half, r], rs.at[half]).start()

    pltpu.make_async_copy(bsend.at[h], b1.at[h], r1).start()
    for i in range(4):
        for j in range(2):
            if i or j:
                d = xs[i] + ys[j] + z
                remote(bsend.at[lax.div(d, 4)], b1.at[h], s1, r1, d, s).start()

    send_rows(0, partners)

    pgate[...] = jnp.dot(normed, w[:, 3 * CM :], preferred_element_type=F32).astype(BF16).astype(F32)
    for t in range(2):
        cols = jax.nn.sigmoid(pgate[:, t * 128 : (t + 1) * 128]).reshape(8, 4, I_LOC, 128)
        for a in range(4):
            tile = None
            for k in range(4):
                piece = cols[:, k]
                if (k - a) % 4:
                    piece = pltpu.roll(piece, (k - a) % 4 * 32, 2)
                tile = piece if tile is None else jnp.where(in_slot(lane3, k), piece, tile)
            for g in range(4):
                for half in range(2):
                    gate[half, t * 4 + a, g] = tile[g * 2 + half]

    pltpu.make_async_copy(bsend, b1, r1).wait()
    for k in range(HEADS):
        b2[k] = b1[k, 0]
    for k in range(4):
        b2[8 + k] = jnp.where(
            low24, b1[2 * k, 1].astype(F32), b1[2 * k + 1, 1].astype(F32)
        ).astype(BF16)
    slot = s * 4 + z
    mine2 = lax.div(s, 2) * 4 + z
    own2 = pltpu.make_async_copy(b2, br.at[slot], loc.at[0])
    own2.start()
    for k in range(1, 8):
        zz, q = zs[k // 2], seqs[k % 2 * 2]
        remote(b2, br.at[slot], s2, r2.at[mine2], h * 4 + zz, q).start()
    remote(b2, br.at[slot], s3, r3.at[z], r, s_c).start()

    loads[2].wait()
    loads[3].wait()
    for hh in range(HEADS):
        for k in range(4):
            wrep[hh * 128 + k * 32 : hh * 128 + (k + 1) * 32, :] = wmix[hh * HD : (hh + 1) * HD, :]
    wfac[...] = jnp.concatenate([wfac_t[...], jnp.zeros((64, CM), BF16)], axis=0)
    for e in range(OPM):
        t = tmat[pl.ds(e, OPM, stride=OPM), :]
        head = t.astype(BF16)
        tcat[e * 32 : (e + 1) * 32, 0:128] = head
        tcat[e * 32 : (e + 1) * 32, 128:256] = (t - head.astype(F32)).astype(BF16)
    acc[...] = jnp.zeros_like(acc)
    amino_row = amino[...].reshape(1, RES)
    poly_row = poly[...].reshape(1, RES)

    def column(row, n):
        tile = row[:, n * 128 : (n + 1) * 128].astype(F32)
        return jnp.transpose(jnp.broadcast_to(tile, (128, 128)), (1, 0))

    amino_col = [column(amino_row, n) for n in range(6)]
    for n in range(6):
        fac[n * 128 : (n + 1) * 128, :] = column(poly_row, n)

    remote(br.at[pl.ds(0, 7)], br.at[pl.ds(0, 7)], s2, r1, r, s_c).wait_send()
    send_rows(1, partners)

    shift = shifts[h]
    poly_f = poly_row.astype(F32)

    def build(zz, pair_n):
        for parity in range(2):
            hh = 2 * pair_n + parity
            row = pl.multiple_of((hh * 4 + zz) * I_LOC, 8)
            own = fac[pl.ds(row, I_LOC), :]
            full = [br[q * 4 + zz, hh].astype(F32) for q in range(4)]
            part = [br[q * 4 + zz, 8 + pair_n].astype(F32) for q in range(4)]
            for q in range(4):
                if q % 2 != parity:
                    part[q] = pltpu.roll(part[q], 64, 1)
            tiles = [
                full[0], jnp.where(low24, part[0], part[1]), full[1],
                full[2], jnp.where(low24, part[2], part[3]), full[3],
            ]
            for n in range(6):
                cols = slice(n * 128, (n + 1) * 128)
                val = tiles[n] + jnp.where(own != poly_f[:, cols], shift, F32(0.0))
                val = jnp.where(amino_row[:, cols] > 0, val * F32(LOG2E), F32(-1e9))
                bias[pl.ds(row, I_LOC), cols] = val

    def finish_z(zz):
        remote(br.at[pl.ds(0, 2)], br.at[pl.ds(0, 2)], s3, r3.at[zz], r, s_c).wait_recv()

        def step(pair_n, c):
            build(zz, pair_n)
            return c

        lax.fori_loop(0, 4, step, 0)

    own2.wait()
    before = None
    for k in (0, 3, 2, 1):
        for y in range(2):
            if k or y:
                zz, q = zs[k], seqs[2 * y]
                at = q * 4 + zz
                remote(
                    b2, br.at[at], s2, r2.at[lax.div(q, 2) * 4 + zz], h * 4 + zz, q
                ).wait_recv()
                remote(br.at[at], br.at[at], s3, r3.at[zz], r, s_c).start()
        if before is not None:
            finish_z(before)
        before = zs[k]
    finish_z(before)

    lane_q = lane_iota((Q_CHUNK, 128))
    lane = lane_iota((RES, 128))
    for half in range(2):
        pltpu.make_async_copy(recv.at[half], recv.at[half], rs.at[half]).wait()
        qs[...] = recv[half, :, 0].astype(F32).reshape(RES, 128).astype(BF16)
        kf = recv[half, :, 1].astype(F32).reshape(RES, 128)
        for n in range(6):
            rows = slice(n * 128, (n + 1) * 128)
            ks[rows, :] = jnp.where(amino_col[n] > 0, kf[rows], F32(0.0)).astype(BF16)
        vs[...] = recv[half, :, 2].astype(F32).reshape(RES, 128).astype(BF16)

        def one_row(rr):
            slot = in_slot(lane, rr)
            xv = jnp.where(slot, vs[...].astype(F32), F32(1.0)).astype(BF16)
            xk = ks[...]
            slot_q = in_slot(lane_q, rr)
            for q0 in range(0, RES, Q_CHUNK):
                rows = slice(q0, q0 + Q_CHUNK)
                xq = jnp.where(slot_q, qs[rows, :].astype(F32), F32(0.0)).astype(BF16)
                o = m = None
                for k0 in range(0, RES, K_CHUNK):
                    keys = slice(k0, k0 + K_CHUNK)
                    sc = nt_dot(xq, xk[keys]) + bias[rows, keys]
                    m1 = jnp.max(sc, axis=-1, keepdims=True)
                    p = jnp.exp2(sc - m1).astype(BF16)
                    o1 = jnp.dot(p, xv[keys], preferred_element_type=F32)
                    if o is None:
                        o, m = o1, m1
                    else:
                        top = jnp.maximum(m, m1)
                        o = o * jnp.exp2(m - top) + o1 * jnp.exp2(m1 - top)
                        m = top
                o = o / pltpu.roll(o, 32, 1)
                acc[half, rows, :] = jnp.where(slot_q, o, acc[half, rows, :])

        def two_rows(rr, c):
            one_row(2 * rr)
            one_row(2 * rr + 1)
            return c

        lax.fori_loop(0, 2, two_rows, 0)
        ret[half] = acc[half].reshape(N_RES, I_LOC, 128).astype(BF16)
        pltpu.make_async_copy(ret.at[half, r], back.at[half, r], rb.at[half]).start()

        for d in partners:
            remote(ret.at[half, d], back.at[half, r], sb.at[half], rb.at[half], d, s).start()

    def send_left(half):
        pltpu.make_async_copy(lbuf.at[half], lall.at[s, half], rl).start()
        for k in range(1, N_SEQ):
            remote(lbuf.at[half], lall.at[s, half], sl, rl, r, seqs[k]).start()

    blk_r = lax.rem(r, 8)

    def send_x(half):
        block = xbuf.at[half, b]
        for k in range(1, 4):
            remote(block, block, sx.at[half], rx.at[half], xs[k] + ys[0] + zs[0], s).start()

    def wait_x(half):
        three = xbuf.at[half, pl.ds(0, 3)]
        remote(three, three, sx.at[half], rx.at[half], r, s_c).wait_recv()

    def send_right(half, k, group):
        dy, dz = YZ[k // 4]
        x = seqs[k % 4]
        src, dst, sem = xbuf.at[half, x], rall.at[blk_r, s, half], rr_sem.at[blk_r]
        if k:
            remote(src, dst, sr.at[group], sem, 8 * b + ys[dy] + zs[dz], x).start()
        else:
            pltpu.make_async_copy(src, dst, sem).start()

    lane16 = lane_iota((16, 128))
    lane96 = lane_iota((4 * I_LOC, 128))
    for n in range(6):
        tr[n * 128 : (n + 1) * 128, :] = amino_col[n]
    own_live = tr[pl.ds(pl.multiple_of(r * I_LOC, 8), I_LOC), :]
    for half in range(2):
        pltpu.make_async_copy(back.at[half], back.at[half], rb.at[half]).wait()
        heads = [
            (back[half, 4 * hh : 4 * hh + 4].astype(F32) * gate[half, hh]).reshape(4 * I_LOC, 128)
            for hh in range(HEADS)
        ]
        gated = jnp.concatenate(
            [
                jnp.concatenate(
                    [jnp.where(in_slot(lane96, k), t, F32(0.0)).astype(BF16) for t in heads], axis=1
                )
                for k in range(4)
            ],
            axis=0,
        )
        delta = jnp.dot(gated, wrep[...], preferred_element_type=F32).reshape(16, I_LOC, CM)
        fams = []
        for k in range(4):
            for g in range(4):
                row = g * 8 + half * 4 + k
                step = live[s * S_LOC + row].astype(F32) * delta[k * 4 + g]
                dbuf[row] = step
                fams.append(msa[row] + step)
        y = layer_norm(jnp.concatenate(fams, axis=0)).astype(BF16)
        f = nt_dot(y, wfac[...])
        for k in range(4):
            for g in range(4):
                on = live[s * S_LOC + g * 8 + half * 4 + k].astype(F32)
                at = (k * 4 + g) * I_LOC
                fac[at : at + I_LOC, :] = f[at : at + I_LOC] * (on * own_live)
        for i0 in range(0, I_LOC, 4):
            tile = None
            for k in range(4):
                i = i0 + k
                f = fac[pl.ds(i, 16, stride=I_LOC), :]
                moved = pltpu.roll(f, k * 32, 1) if k else f
                tile = moved if tile is None else jnp.where(in_slot(lane16, k), moved, tile)
                ft = jnp.transpose(f, (1, 0))[OPM : 2 * OPM, :]
                tr[i * OPM : (i + 1) * OPM, :] = jnp.concatenate(
                    [ft, jnp.zeros((OPM, 112), F32)], axis=1
                )
            lbuf[half, :, i0 * 32 : (i0 + 4) * 32] = tile.astype(BF16)
        send_left(half)
        for e0 in range(0, OPM, 8):
            tile = tr[pl.ds(e0, I_LOC, stride=OPM), :]
            for k in range(1, 8):
                moved = pltpu.roll(tr[pl.ds(e0 + k, I_LOC, stride=OPM), :], k * 16, 1)
                tile = jnp.where(lane24 >= k * 16, moved, tile)
            xbuf[half, b, :, e0 * 16 : (e0 + 8) * 16] = tile.astype(BF16)
        send_x(half)
        wait_x(half)
        if half == 0:
            for k in range(16):
                send_right(0, k, 4)
        else:
            for k in range(8):
                send_right(1, k, 0)
            out_delta = pltpu.make_async_copy(dbuf, delta_hbm, outs.at[16])
            out_delta.start()

    def take_left():
        pltpu.make_async_copy(lall, lall, rl).wait()
        left = lall[...].reshape(N_SEQ * S_LOC, I_LOC * OPM)
        for n in range(6):
            lw[n] = left[:, n * 128 : (n + 1) * 128]

    def wait_sent(group, blocks):
        for size, ref in ((8, rall.at[0]), (2, rall.at[0, 0]), (1, rall.at[0, 0, 0])):
            for _ in range(blocks // size):
                remote(ref, ref, sr.at[group], r1, r, s_c).wait_send()
            blocks %= size

    def send_group(group):
        for k in range(8 * group, 8 * group + 8):
            send_right(0, k, group)
            send_right(1, k, group)

    count = lax.fori_loop(0, 128, lambda k, c: c + live[k], jnp.int32(0)).astype(F32)
    inv = 1.0 / jnp.maximum(jnp.full((1, 128), count, F32), 1.0)

    wait_sent(0, 7)
    for k in range(8, 16):
        send_right(1, k, 1)
    send_group(2)

    def blocks_of(c):
        blocks = []
        for t in range(J_BLOCKS):
            kk = lax.rem((c * J_BLOCKS + t) * 3, 8)
            blocks.append(
                lax.rem(y_lo + 2 - lax.div(kk, 4), 2) * 4 + lax.rem(z + 4 - lax.rem(kk, 4), 4)
            )
        return blocks

    def result(c, t, p, blk):
        some = pl.ds(12 * p, 12)
        return pltpu.make_async_copy(
            pbuf.at[blk, some],
            proj_hbm.at[some, pl.ds(pl.multiple_of(blk * I_LOC, 8), I_LOC)],
            outs.at[c * 4 + t * 2 + p],
        )

    def one_chunk(c, carry):
        blocks = blocks_of(c)
        for blk in blocks:
            pltpu.make_async_copy(rall.at[blk], rall.at[blk], rr_sem.at[blk]).wait()
        for ge in range(4):
            cols = slice(ge * 128, (ge + 1) * 128)
            tiles = [
                jnp.concatenate([rall[blk, q, half, :, cols].astype(F32) for blk in blocks], axis=0)
                for q in range(N_SEQ)
                for half in range(2)
            ]
            for e, tile in enumerate(exchange_lanes(tiles, 16)):
                lhs[(ge * 8 + e) * JC : (ge * 8 + e + 1) * JC, :] = tile.astype(BF16)

        @pl.when(c == 0)
        def _():
            wait_sent(1, 8)
            send_group(3)
            take_left()

        def spread(p, cc):
            w2 = jnp.concatenate([lw[2 * p], lw[2 * p + 1]], axis=1)
            o = jnp.dot(lhs[...], w2, preferred_element_type=F32).astype(BF16)
            for t in range(2):
                for g in range(8):
                    tiles = [
                        o[(4 * g + k) * JC : (4 * g + k + 1) * JC, t * 128 : (t + 1) * 128]
                        for k in range(4)
                    ]
                    for m, tile in enumerate(exchange_lanes(tiles, 32)):
                        amat[(2 * p + t) * 4 + m, :, g * 128 : (g + 1) * 128] = tile
            return cc

        lax.fori_loop(0, 3, spread, 0)

        def finish(p, cc):
            some = pl.ds(12 * p, 12)
            o = jnp.dot(amat[some].reshape(12 * JC, 1024), tcat[...], preferred_element_type=F32)
            o = ((o[:, :128] + o[:, 128:]) * inv).reshape(12, JC, CZ)
            for t, blk in enumerate(blocks):
                pbuf[blk, some] = o[:, t * I_LOC : (t + 1) * I_LOC]
                result(c, t, p, blk).start()
            return cc

        lax.fori_loop(0, 2, finish, 0)
        return carry

    lax.fori_loop(0, 8 // J_BLOCKS, one_chunk, 0)

    out_delta.wait()

    def result_out(c, carry):
        for t, blk in enumerate(blocks_of(c)):
            for p in range(2):
                result(c, t, p, blk).wait()
        return carry

    lax.fori_loop(0, 8 // J_BLOCKS, result_out, 0)
    remote(bsend.at[pl.ds(0, 7)], b1.at[pl.ds(0, 7)], s1, r1, r, s_c).wait_send()
    remote(br.at[pl.ds(0, 8)], br.at[pl.ds(0, 8)], s3, r1, r, s_c).wait_send()
    remote(qsend.at[pl.ds(0, 31)], qsend.at[pl.ds(0, 31)], ss, r1, r, s_c).wait_send()
    for half in range(2):
        remote(
            ret.at[half, pl.ds(0, 31)], ret.at[half, pl.ds(0, 31)], sb.at[half], r1, r, s_c
        ).wait_send()
    remote(lall.at[pl.ds(0, 3)], lall.at[pl.ds(0, 3)], sl, r1, r, s_c).wait_send()
    wait_sent(2, 16)
    wait_sent(3, 16)
    wait_sent(4, 15)
    for half in range(2):
        three = xbuf.at[half, pl.ds(0, 3)]
        remote(three, three, sx.at[half], r1, r, s_c).wait_send()


def on_device(msa, pair, amino, poly, live, w, wshift, shifts, wmix, wfac, tmat):
    dma = pltpu.SemaphoreType.DMA
    vm = pl.BlockSpec(memory_space=pltpu.VMEM)
    sm = pl.BlockSpec(memory_space=pltpu.SMEM)
    hbm = pl.BlockSpec(memory_space=pl.ANY)
    delta, proj = pl.pallas_call(
        kernel,
        out_shape=(
            jax.ShapeDtypeStruct((S_LOC, I_LOC, CM), F32),
            jax.ShapeDtypeStruct((I_LOC, J_LOC, CZ), F32),
        ),
        in_specs=[hbm] * 5 + [vm] * 4 + [sm] * 2,
        out_specs=(hbm, hbm),
        scratch_shapes=[
            pltpu.VMEM((S_LOC, I_LOC, CM), F32),
            pltpu.VMEM((I_LOC, J_LOC, CZ), F32),
            pltpu.VMEM((CM, 4 * CM), BF16),
            pltpu.VMEM((CM, CM), BF16),
            pltpu.VMEM((OPM * OPM, CZ), F32),
            pltpu.VMEM((S_LOC, I_LOC, CM), F32),
            pltpu.VMEM((8, I_LOC, I_LOC, CZ), F32),
            pltpu.VMEM((2, I_LOC * HEADS, 128), F32),
            pltpu.VMEM((HEADS, 2, I_LOC, 128), BF16),
            pltpu.VMEM((HEADS, 2, I_LOC, 128), BF16),
            pltpu.VMEM((12, I_LOC, 128), BF16),
            pltpu.VMEM((N_SEQ * 4, 12, I_LOC, 128), BF16),
            pltpu.VMEM((RES, RES), F32),
            pltpu.VMEM((RES, CM), F32),
            pltpu.VMEM((2, HEADS, 4, I_LOC, 128), F32),
            pltpu.VMEM((N_RES, 2, 3, I_LOC, 128), BF16),
            pltpu.VMEM((2, N_RES, 3, I_LOC, 128), BF16),
            pltpu.VMEM((RES, 128), BF16),
            pltpu.VMEM((RES, 128), BF16),
            pltpu.VMEM((RES, 128), BF16),
            pltpu.VMEM((2, RES, 128), F32),
            pltpu.VMEM((2, N_RES, I_LOC, 128), BF16),
            pltpu.VMEM((2, N_RES, I_LOC, 128), BF16),
            pltpu.VMEM((1024, CM), BF16),
            pltpu.VMEM((128, CM), BF16),
            pltpu.VMEM((RES, 128), F32),
            pltpu.VMEM((I_LOC * OPM, 128), F32),
            pltpu.VMEM((2, 16, I_LOC * OPM), BF16),
            pltpu.VMEM((2, 4, I_LOC, OPM * 16), BF16),
            pltpu.VMEM((N_SEQ, 2, 16, I_LOC * OPM), BF16),
            pltpu.VMEM((8, N_SEQ, 2, I_LOC, OPM * 16), BF16),
            pltpu.VMEM((6, N_SEQ * S_LOC, 128), BF16),
            pltpu.VMEM((1024, 256), BF16),
            pltpu.VMEM((OPM * JC, 128), BF16),
            pltpu.VMEM((I_LOC, JC, 1024), BF16),
            dma, dma((2,)), dma, dma, dma, dma((8,)), dma, dma((4,)),
            dma((2,)), dma((2,)), dma, dma, dma((2,)), dma((2,)),
            dma((5,)), dma((8,)), dma((1,)),
            dma((10,)), dma((17,)),
        ],
        compiler_params=pltpu.CompilerParams(
            collective_id=0, has_side_effects=True, vmem_limit_bytes=VMEM_LIMIT
        ),
        name="evoformer",
    )(msa, pair, w, wmix, tmat, amino, poly, wshift.T, wfac.T, live, shifts)
    return msa + delta, pair + proj


def solution(mesh):
    in_specs = (P("seq", "res", None), P("res", "seq", None)) + (P(),) * 9
    out_specs = (P("seq", "res", None), P("res", "seq", None))
    return jax.shard_map(
        on_device, mesh=mesh, in_specs=in_specs, out_specs=out_specs, check_vma=False
    )
```

```python
import math

import jax
import jax.numpy as jnp
from jax import lax
from jax.experimental import pallas as pl
from jax.experimental.pallas import tpu as pltpu
from jax.sharding import PartitionSpec as P

MESH = pl.DeviceIdType.MESH
F32 = jnp.float32
BF16 = jnp.bfloat16
LOG2E = math.log2(math.e)
VMEM_LIMIT = 58 * 1024 * 1024

N_RES, N_SEQ = 32, 4
S_LOC, I_LOC, J_LOC = 32, 24, 192
CM, CZ, HEADS, HD, OPM = 256, 128, 8, 32, 32
RES = 768
Q_CHUNK, K_CHUNK = 384, 256
OFFSETS = [((k * 11) % 32 // 8, (k * 11) % 8 // 4, (k * 11) % 4) for k in range(1, N_RES)]
YZ = [((k * 3) % 8 // 4, (k * 3) % 4) for k in range(8)]
J_BLOCKS = 2
JC = J_BLOCKS * I_LOC


def lane_iota(shape):
    return lax.broadcasted_iota(jnp.int32, shape, len(shape) - 1)


def in_slot(lane, k):
    return (lane >= k * 32) & (lane < (k + 1) * 32)


def layer_norm(x):
    centre = jnp.mean(x, axis=-1, keepdims=True)
    d = x - centre
    spread = jnp.mean(d * d, axis=-1, keepdims=True)
    return d * lax.rsqrt(spread + 1e-05)


def nt_dot(a, b, precision=None):
    return lax.dot_general(
        a, b, (((1,), (1,)), ((), ())), precision=precision, preferred_element_type=F32
    )


def exchange_lanes(tiles, width):
    lane = lane_iota(tiles[0].shape)
    tiles, bit = list(tiles), 1
    while bit < len(tiles):
        low = lax.rem(lane, 2 * bit * width) < bit * width
        new = list(tiles)
        for k in range(len(tiles)):
            if not k & bit:
                a, b = tiles[k], tiles[k | bit]
                new[k] = jnp.where(low, a, pltpu.roll(b, bit * width, 1))
                new[k | bit] = jnp.where(low, pltpu.roll(a, 128 - bit * width, 1), b)
        tiles, bit = new, 2 * bit
    return tiles


def remote(src, dst, a, b, d, q):
    return pltpu.make_async_remote_copy(
        src_ref=src, dst_ref=dst, send_sem=a, recv_sem=b, device_id=(d, q), device_id_type=MESH
    )


def kernel(
    msa_hbm, pair_hbm, w_hbm, wmix_hbm, tmat_hbm, amino, poly, wshift_t, wfac_t, live, shifts,
    delta_hbm, proj_hbm,
    msa, pair, w, wmix, tmat, dbuf, pbuf,
    btmp, bsend, b1, b2, br, bias, pgate, gate, qsend, recv, qs, ks, vs, acc, ret, back,
    wrep, wfac, fac, tr, lbuf, xbuf, lall, rall, lw, tcat, lhs, amat,
    ss, rs, s1, r1, s2, r2, s3, r3, sb, rb, sl, rl, sx, rx, sr, rr_sem, loc, ins, outs,
):
    r, s = lax.axis_index("res"), lax.axis_index("seq")
    h, z = lax.div(r, 4), lax.rem(r, 4)
    y_lo, b = lax.rem(h, 2), lax.div(r, 8)
    s_c = s + 1 - 2 * lax.rem(s, 2)
    xs = [lax.rem(b + k, 4) * 8 for k in range(4)]
    ys = [lax.rem(y_lo + k, 2) * 4 for k in range(2)]
    zs = [lax.rem(z + k, 4) for k in range(4)]
    seqs = [lax.rem(s + k, 4) for k in range(4)]
    partners = [xs[i] + ys[j] + zs[k] for i, j, k in OFFSETS]

    loads = [
        pltpu.make_async_copy(src, dst, ins.at[6 + n])
        for n, (src, dst) in enumerate(
            ((msa_hbm, msa), (w_hbm, w), (wmix_hbm, wmix), (tmat_hbm, tmat))
        )
    ]
    pair_loads = [
        pltpu.make_async_copy(pair_hbm.at[pl.ds(4 * n, 4)], pair.at[pl.ds(4 * n, 4)], ins.at[n])
        for n in range(6)
    ]
    for cp in loads[:2] + pair_loads + loads[2:]:
        cp.start()

    barrier = pltpu.get_barrier_semaphore()

    def greet(d, q):
        pl.semaphore_signal(barrier, inc=1, device_id=(d, q), device_id_type=MESH)

    for d in partners:
        greet(d, s)
    for k in range(4):
        greet(h * 4 + k, seqs[2])
    for k in range(1, N_SEQ):
        greet(r, seqs[k])
    for dy, dz in YZ:
        for k in range(N_SEQ):
            if dy or dz or k:
                greet(8 * b + ys[dy] + zs[dz], seqs[k])

    loads[0].wait()
    loads[1].wait()
    normed = layer_norm(msa[...].reshape(S_LOC * I_LOC, CM)).astype(BF16)
    lane3 = lane_iota((8, I_LOC, 128))
    for part in range(3):
        out = jnp.dot(normed, w[:, part * CM : (part + 1) * CM], preferred_element_type=F32)
        if part == 0:
            out = out * F32(LOG2E / math.sqrt(HD))
        for t in range(2):
            cols = out[:, t * 128 : (t + 1) * 128].reshape(8, 4, I_LOC, 128)
            for a in range(4):
                tile = None
                for k in range(4):
                    piece = cols[:, k]
                    if (k - a) % 4:
                        piece = pltpu.roll(piece, (k - a) % 4 * 32, 2)
                    tile = piece if tile is None else jnp.where(in_slot(lane3, k), piece, tile)
                tile = tile.astype(BF16)
                for g in range(4):
                    for half in range(2):
                        qsend[(t * 4 + a) * 4 + g, half, part] = tile[g * 2 + half]

    btmp[...] = jnp.zeros_like(btmp)
    chunk = 4
    for cp in pair_loads:
        cp.wait()
    for i0 in range(0, I_LOC, chunk):
        zn = layer_norm(pair[i0 : i0 + chunk].reshape(chunk * J_LOC, CZ))
        bb = nt_dot(wshift_t[...], zn, lax.Precision.HIGHEST)
        for i in range(chunk):
            rows, col = slice((i0 + i) * HEADS, (i0 + i + 1) * HEADS), i * J_LOC
            btmp[0, rows, :] = bb[:, col : col + 128]
            btmp[1, rows, 0:64] = bb[:, col + 128 : col + J_LOC]
    odd = jnp.full((I_LOC, 128), lax.rem(s, 2), jnp.int32) > 0
    swap = jnp.full((I_LOC, 128), lax.rem(h, 2), jnp.int32) > 0
    lane24 = lane_iota((I_LOC, 128))
    low24 = lane24 < 64
    for hh in range(HEADS):
        v0, v1 = (btmp[n, pl.ds(hh, I_LOC, stride=HEADS), :] for n in range(2))
        t0, t1 = pltpu.roll(v0, 64, 1), pltpu.roll(v1, 64, 1)
        bsend[hh, 0] = jnp.where(odd, jnp.where(low24, t0, t1), v0).astype(BF16)
        part = jnp.where(odd, v0, v1)
        bsend[hh, 1] = jnp.where(swap, pltpu.roll(part, 64, 1), part).astype(BF16)

    pl.semaphore_wait(barrier, 31 + 4 + 3 + 31)

    def send_rows(half, some):
        for d in some:
            remote(qsend.at[d, half], recv.at[half, r], ss, rs.at[half], d, s).start()

    for half in range(2):
        pltpu.make_async_copy(qsend.at[r, half], recv.at[half, r], rs.at[half]).start()

    pltpu.make_async_copy(bsend.at[h], b1.at[h], r1).start()
    for i in range(4):
        for j in range(2):
            if i or j:
                d = xs[i] + ys[j] + z
                remote(bsend.at[lax.div(d, 4)], b1.at[h], s1, r1, d, s).start()

    send_rows(0, partners)

    pgate[...] = jnp.dot(normed, w[:, 3 * CM :], preferred_element_type=F32).astype(BF16).astype(F32)
    for t in range(2):
        cols = jax.nn.sigmoid(pgate[:, t * 128 : (t + 1) * 128]).reshape(8, 4, I_LOC, 128)
        for a in range(4):
            tile = None
            for k in range(4):
                piece = cols[:, k]
                if (k - a) % 4:
                    piece = pltpu.roll(piece, (k - a) % 4 * 32, 2)
                tile = piece if tile is None else jnp.where(in_slot(lane3, k), piece, tile)
            for g in range(4):
                for half in range(2):
                    gate[half, t * 4 + a, g] = tile[g * 2 + half]

    pltpu.make_async_copy(bsend, b1, r1).wait()
    for k in range(HEADS):
        b2[k] = b1[k, 0]
    for k in range(4):
        b2[8 + k] = jnp.where(
            low24, b1[2 * k, 1].astype(F32), b1[2 * k + 1, 1].astype(F32)
        ).astype(BF16)
    slot = s * 4 + z
    mine2 = lax.div(s, 2) * 4 + z
    own2 = pltpu.make_async_copy(b2, br.at[slot], loc.at[0])
    own2.start()
    for k in range(1, 8):
        zz, q = zs[k // 2], seqs[k % 2 * 2]
        remote(b2, br.at[slot], s2, r2.at[mine2], h * 4 + zz, q).start()
    remote(b2, br.at[slot], s3, r3.at[z], r, s_c).start()

    loads[2].wait()
    loads[3].wait()
    for hh in range(HEADS):
        for k in range(4):
            wrep[hh * 128 + k * 32 : hh * 128 + (k + 1) * 32, :] = wmix[hh * HD : (hh + 1) * HD, :]
    wfac[...] = jnp.concatenate([wfac_t[...], jnp.zeros((64, CM), BF16)], axis=0)
    for e in range(OPM):
        t = tmat[pl.ds(e, OPM, stride=OPM), :]
        head = t.astype(BF16)
        tcat[e * 32 : (e + 1) * 32, 0:128] = head
        tcat[e * 32 : (e + 1) * 32, 128:256] = (t - head.astype(F32)).astype(BF16)
    acc[...] = jnp.zeros_like(acc)
    amino_row = amino[...].reshape(1, RES)
    poly_row = poly[...].reshape(1, RES)

    def column(row, n):
        tile = row[:, n * 128 : (n + 1) * 128].astype(F32)
        return jnp.transpose(jnp.broadcast_to(tile, (128, 128)), (1, 0))

    amino_col = [column(amino_row, n) for n in range(6)]
    for n in range(6):
        fac[n * 128 : (n + 1) * 128, :] = column(poly_row, n)

    remote(br.at[pl.ds(0, 7)], br.at[pl.ds(0, 7)], s2, r1, r, s_c).wait_send()
    send_rows(1, partners)

    shift = shifts[h]
    poly_f = poly_row.astype(F32)

    def build(zz, pair_n):
        for parity in range(2):
            hh = 2 * pair_n + parity
            row = pl.multiple_of((hh * 4 + zz) * I_LOC, 8)
            own = fac[pl.ds(row, I_LOC), :]
            full = [br[q * 4 + zz, hh].astype(F32) for q in range(4)]
            part = [br[q * 4 + zz, 8 + pair_n].astype(F32) for q in range(4)]
            for q in range(4):
                if q % 2 != parity:
                    part[q] = pltpu.roll(part[q], 64, 1)
            tiles = [
                full[0], jnp.where(low24, part[0], part[1]), full[1],
                full[2], jnp.where(low24, part[2], part[3]), full[3],
            ]
            for n in range(6):
                cols = slice(n * 128, (n + 1) * 128)
                val = tiles[n] + jnp.where(own != poly_f[:, cols], shift, F32(0.0))
                val = jnp.where(amino_row[:, cols] > 0, val * F32(LOG2E), F32(-1e9))
                bias[pl.ds(row, I_LOC), cols] = val

    def finish_z(zz):
        remote(br.at[pl.ds(0, 2)], br.at[pl.ds(0, 2)], s3, r3.at[zz], r, s_c).wait_recv()

        def step(pair_n, c):
            build(zz, pair_n)
            return c

        lax.fori_loop(0, 4, step, 0)

    own2.wait()
    before = None
    for k in (0, 3, 2, 1):
        for y in range(2):
            if k or y:
                zz, q = zs[k], seqs[2 * y]
                at = q * 4 + zz
                remote(
                    b2, br.at[at], s2, r2.at[lax.div(q, 2) * 4 + zz], h * 4 + zz, q
                ).wait_recv()
                remote(br.at[at], br.at[at], s3, r3.at[zz], r, s_c).start()
        if before is not None:
            finish_z(before)
        before = zs[k]
    finish_z(before)

    lane_q = lane_iota((Q_CHUNK, 128))
    lane = lane_iota((RES, 128))
    for half in range(2):
        pltpu.make_async_copy(recv.at[half], recv.at[half], rs.at[half]).wait()
        qs[...] = recv[half, :, 0].astype(F32).reshape(RES, 128).astype(BF16)
        kf = recv[half, :, 1].astype(F32).reshape(RES, 128)
        for n in range(6):
            rows = slice(n * 128, (n + 1) * 128)
            ks[rows, :] = jnp.where(amino_col[n] > 0, kf[rows], F32(0.0)).astype(BF16)
        vs[...] = recv[half, :, 2].astype(F32).reshape(RES, 128).astype(BF16)

        def one_row(rr):
            slot = in_slot(lane, rr)
            xv = jnp.where(slot, vs[...].astype(F32), F32(1.0)).astype(BF16)
            xk = ks[...]
            slot_q = in_slot(lane_q, rr)
            for q0 in range(0, RES, Q_CHUNK):
                rows = slice(q0, q0 + Q_CHUNK)
                xq = jnp.where(slot_q, qs[rows, :].astype(F32), F32(0.0)).astype(BF16)
                o = m = None
                for k0 in range(0, RES, K_CHUNK):
                    keys = slice(k0, k0 + K_CHUNK)
                    sc = nt_dot(xq, xk[keys]) + bias[rows, keys]
                    m1 = jnp.max(sc, axis=-1, keepdims=True)
                    p = jnp.exp2(sc - m1).astype(BF16)
                    o1 = jnp.dot(p, xv[keys], preferred_element_type=F32)
                    if o is None:
                        o, m = o1, m1
                    else:
                        top = jnp.maximum(m, m1)
                        o = o * jnp.exp2(m - top) + o1 * jnp.exp2(m1 - top)
                        m = top
                o = o / pltpu.roll(o, 32, 1)
                acc[half, rows, :] = jnp.where(slot_q, o, acc[half, rows, :])

        def two_rows(rr, c):
            one_row(2 * rr)
            one_row(2 * rr + 1)
            return c

        lax.fori_loop(0, 2, two_rows, 0)
        ret[half] = acc[half].reshape(N_RES, I_LOC, 128).astype(BF16)
        pltpu.make_async_copy(ret.at[half, r], back.at[half, r], rb.at[half]).start()

        for d in partners:
            remote(ret.at[half, d], back.at[half, r], sb.at[half], rb.at[half], d, s).start()

    def send_left(half):
        pltpu.make_async_copy(lbuf.at[half], lall.at[s, half], rl).start()
        for k in range(1, N_SEQ):
            remote(lbuf.at[half], lall.at[s, half], sl, rl, r, seqs[k]).start()

    blk_r = lax.rem(r, 8)

    def send_x(half):
        block = xbuf.at[half, b]
        for k in range(1, 4):
            remote(block, block, sx.at[half], rx.at[half], xs[k] + ys[0] + zs[0], s).start()

    def wait_x(half):
        three = xbuf.at[half, pl.ds(0, 3)]
        remote(three, three, sx.at[half], rx.at[half], r, s_c).wait_recv()

    def send_right(half, k, group):
        dy, dz = YZ[k // 4]
        x = seqs[k % 4]
        src, dst, sem = xbuf.at[half, x], rall.at[blk_r, s, half], rr_sem.at[blk_r]
        if k:
            remote(src, dst, sr.at[group], sem, 8 * b + ys[dy] + zs[dz], x).start()
        else:
            pltpu.make_async_copy(src, dst, sem).start()

    lane16 = lane_iota((16, 128))
    lane96 = lane_iota((4 * I_LOC, 128))
    for n in range(6):
        tr[n * 128 : (n + 1) * 128, :] = amino_col[n]
    own_live = tr[pl.ds(pl.multiple_of(r * I_LOC, 8), I_LOC), :]
    for half in range(2):
        pltpu.make_async_copy(back.at[half], back.at[half], rb.at[half]).wait()
        heads = [
            (back[half, 4 * hh : 4 * hh + 4].astype(F32) * gate[half, hh]).reshape(4 * I_LOC, 128)
            for hh in range(HEADS)
        ]
        gated = jnp.concatenate(
            [
                jnp.concatenate(
                    [jnp.where(in_slot(lane96, k), t, F32(0.0)).astype(BF16) for t in heads], axis=1
                )
                for k in range(4)
            ],
            axis=0,
        )
        delta = jnp.dot(gated, wrep[...], preferred_element_type=F32).reshape(16, I_LOC, CM)
        fams = []
        for k in range(4):
            for g in range(4):
                row = g * 8 + half * 4 + k
                step = live[s * S_LOC + row].astype(F32) * delta[k * 4 + g]
                dbuf[row] = step
                fams.append(msa[row] + step)
        y = layer_norm(jnp.concatenate(fams, axis=0)).astype(BF16)
        f = nt_dot(y, wfac[...])
        for k in range(4):
            for g in range(4):
                on = live[s * S_LOC + g * 8 + half * 4 + k].astype(F32)
                at = (k * 4 + g) * I_LOC
                fac[at : at + I_LOC, :] = f[at : at + I_LOC] * (on * own_live)
        for i0 in range(0, I_LOC, 4):
            tile = None
            for k in range(4):
                i = i0 + k
                f = fac[pl.ds(i, 16, stride=I_LOC), :]
                moved = pltpu.roll(f, k * 32, 1) if k else f
                tile = moved if tile is None else jnp.where(in_slot(lane16, k), moved, tile)
                ft = jnp.transpose(f, (1, 0))[OPM : 2 * OPM, :]
                tr[i * OPM : (i + 1) * OPM, :] = jnp.concatenate(
                    [ft, jnp.zeros((OPM, 112), F32)], axis=1
                )
            lbuf[half, :, i0 * 32 : (i0 + 4) * 32] = tile.astype(BF16)
        send_left(half)
        for e0 in range(0, OPM, 8):
            tile = tr[pl.ds(e0, I_LOC, stride=OPM), :]
            for k in range(1, 8):
                moved = pltpu.roll(tr[pl.ds(e0 + k, I_LOC, stride=OPM), :], k * 16, 1)
                tile = jnp.where(lane24 >= k * 16, moved, tile)
            xbuf[half, b, :, e0 * 16 : (e0 + 8) * 16] = tile.astype(BF16)
        send_x(half)
        wait_x(half)
        if half == 0:
            for k in range(16):
                send_right(0, k, 4)
        else:
            for k in range(8):
                send_right(1, k, 0)
            out_delta = pltpu.make_async_copy(dbuf, delta_hbm, outs.at[16])
            out_delta.start()

    def take_left():
        pltpu.make_async_copy(lall, lall, rl).wait()
        left = lall[...].reshape(N_SEQ * S_LOC, I_LOC * OPM)
        for n in range(6):
            lw[n] = left[:, n * 128 : (n + 1) * 128]

    def wait_sent(group, blocks):
        for size, ref in ((8, rall.at[0]), (2, rall.at[0, 0]), (1, rall.at[0, 0, 0])):
            for _ in range(blocks // size):
                remote(ref, ref, sr.at[group], r1, r, s_c).wait_send()
            blocks %= size

    def send_group(group):
        for k in range(8 * group, 8 * group + 8):
            send_right(0, k, group)
            send_right(1, k, group)

    count = lax.fori_loop(0, 128, lambda k, c: c + live[k], jnp.int32(0)).astype(F32)
    inv = 1.0 / jnp.maximum(jnp.full((1, 128), count, F32), 1.0)

    for k in range(8, 16):
        send_right(1, k, 1)

    def blocks_of(c):
        blocks = []
        for t in range(J_BLOCKS):
            kk = lax.rem((c * J_BLOCKS + t) * 3, 8)
            blocks.append(
                lax.rem(y_lo + 2 - lax.div(kk, 4), 2) * 4 + lax.rem(z + 4 - lax.rem(kk, 4), 4)
            )
        return blocks

    def result(c, t, p, blk):
        some = pl.ds(12 * p, 12)
        return pltpu.make_async_copy(
            pbuf.at[blk, some],
            proj_hbm.at[some, pl.ds(pl.multiple_of(blk * I_LOC, 8), I_LOC)],
            outs.at[c * 4 + t * 2 + p],
        )

    def one_chunk(c, carry):
        blocks = blocks_of(c)
        for blk in blocks:
            pltpu.make_async_copy(rall.at[blk], rall.at[blk], rr_sem.at[blk]).wait()
        for ge in range(4):
            cols = slice(ge * 128, (ge + 1) * 128)
            tiles = [
                jnp.concatenate([rall[blk, q, half, :, cols].astype(F32) for blk in blocks], axis=0)
                for q in range(N_SEQ)
                for half in range(2)
            ]
            for e, tile in enumerate(exchange_lanes(tiles, 16)):
                lhs[(ge * 8 + e) * JC : (ge * 8 + e + 1) * JC, :] = tile.astype(BF16)

        @pl.when(c == 0)
        def _():
            send_group(2)
            take_left()

        @pl.when(c == 1)
        def _():
            send_group(3)

        def spread(p, cc):
            w2 = jnp.concatenate([lw[2 * p], lw[2 * p + 1]], axis=1)
            o = jnp.dot(lhs[...], w2, preferred_element_type=F32).astype(BF16)
            for t in range(2):
                for g in range(8):
                    tiles = [
                        o[(4 * g + k) * JC : (4 * g + k + 1) * JC, t * 128 : (t + 1) * 128]
                        for k in range(4)
                    ]
                    for m, tile in enumerate(exchange_lanes(tiles, 32)):
                        amat[(2 * p + t) * 4 + m, :, g * 128 : (g + 1) * 128] = tile
            return cc

        lax.fori_loop(0, 3, spread, 0)

        def finish(p, cc):
            some = pl.ds(12 * p, 12)
            o = jnp.dot(amat[some].reshape(12 * JC, 1024), tcat[...], preferred_element_type=F32)
            o = ((o[:, :128] + o[:, 128:]) * inv).reshape(12, JC, CZ)
            for t, blk in enumerate(blocks):
                pbuf[blk, some] = o[:, t * I_LOC : (t + 1) * I_LOC]
                result(c, t, p, blk).start()
            return cc

        lax.fori_loop(0, 2, finish, 0)
        return carry

    lax.fori_loop(0, 8 // J_BLOCKS, one_chunk, 0)

    out_delta.wait()

    def result_out(c, carry):
        for t, blk in enumerate(blocks_of(c)):
            for p in range(2):
                result(c, t, p, blk).wait()
        return carry

    lax.fori_loop(0, 8 // J_BLOCKS, result_out, 0)
    remote(bsend.at[pl.ds(0, 7)], b1.at[pl.ds(0, 7)], s1, r1, r, s_c).wait_send()
    remote(br.at[pl.ds(0, 8)], br.at[pl.ds(0, 8)], s3, r1, r, s_c).wait_send()
    remote(qsend.at[pl.ds(0, 31)], qsend.at[pl.ds(0, 31)], ss, r1, r, s_c).wait_send()
    for half in range(2):
        remote(
            ret.at[half, pl.ds(0, 31)], ret.at[half, pl.ds(0, 31)], sb.at[half], r1, r, s_c
        ).wait_send()
    remote(lall.at[pl.ds(0, 3)], lall.at[pl.ds(0, 3)], sl, r1, r, s_c).wait_send()
    wait_sent(0, 7)
    wait_sent(1, 8)
    wait_sent(2, 16)
    wait_sent(3, 16)
    wait_sent(4, 15)
    for half in range(2):
        three = xbuf.at[half, pl.ds(0, 3)]
        remote(three, three, sx.at[half], r1, r, s_c).wait_send()


def on_device(msa, pair, amino, poly, live, w, wshift, shifts, wmix, wfac, tmat):
    dma = pltpu.SemaphoreType.DMA
    vm = pl.BlockSpec(memory_space=pltpu.VMEM)
    sm = pl.BlockSpec(memory_space=pltpu.SMEM)
    hbm = pl.BlockSpec(memory_space=pl.ANY)
    delta, proj = pl.pallas_call(
        kernel,
        out_shape=(
            jax.ShapeDtypeStruct((S_LOC, I_LOC, CM), F32),
            jax.ShapeDtypeStruct((I_LOC, J_LOC, CZ), F32),
        ),
        in_specs=[hbm] * 5 + [vm] * 4 + [sm] * 2,
        out_specs=(hbm, hbm),
        scratch_shapes=[
            pltpu.VMEM((S_LOC, I_LOC, CM), F32),
            pltpu.VMEM((I_LOC, J_LOC, CZ), F32),
            pltpu.VMEM((CM, 4 * CM), BF16),
            pltpu.VMEM((CM, CM), BF16),
            pltpu.VMEM((OPM * OPM, CZ), F32),
            pltpu.VMEM((S_LOC, I_LOC, CM), F32),
            pltpu.VMEM((8, I_LOC, I_LOC, CZ), F32),
            pltpu.VMEM((2, I_LOC * HEADS, 128), F32),
            pltpu.VMEM((HEADS, 2, I_LOC, 128), BF16),
            pltpu.VMEM((HEADS, 2, I_LOC, 128), BF16),
            pltpu.VMEM((12, I_LOC, 128), BF16),
            pltpu.VMEM((N_SEQ * 4, 12, I_LOC, 128), BF16),
            pltpu.VMEM((RES, RES), F32),
            pltpu.VMEM((RES, CM), F32),
            pltpu.VMEM((2, HEADS, 4, I_LOC, 128), F32),
            pltpu.VMEM((N_RES, 2, 3, I_LOC, 128), BF16),
            pltpu.VMEM((2, N_RES, 3, I_LOC, 128), BF16),
            pltpu.VMEM((RES, 128), BF16),
            pltpu.VMEM((RES, 128), BF16),
            pltpu.VMEM((RES, 128), BF16),
            pltpu.VMEM((2, RES, 128), F32),
            pltpu.VMEM((2, N_RES, I_LOC, 128), BF16),
            pltpu.VMEM((2, N_RES, I_LOC, 128), BF16),
            pltpu.VMEM((1024, CM), BF16),
            pltpu.VMEM((128, CM), BF16),
            pltpu.VMEM((RES, 128), F32),
            pltpu.VMEM((I_LOC * OPM, 128), F32),
            pltpu.VMEM((2, 16, I_LOC * OPM), BF16),
            pltpu.VMEM((2, 4, I_LOC, OPM * 16), BF16),
            pltpu.VMEM((N_SEQ, 2, 16, I_LOC * OPM), BF16),
            pltpu.VMEM((8, N_SEQ, 2, I_LOC, OPM * 16), BF16),
            pltpu.VMEM((6, N_SEQ * S_LOC, 128), BF16),
            pltpu.VMEM((1024, 256), BF16),
            pltpu.VMEM((OPM * JC, 128), BF16),
            pltpu.VMEM((I_LOC, JC, 1024), BF16),
            dma, dma((2,)), dma, dma, dma, dma((8,)), dma, dma((4,)),
            dma((2,)), dma((2,)), dma, dma, dma((2,)), dma((2,)),
            dma((5,)), dma((8,)), dma((1,)),
            dma((10,)), dma((17,)),
        ],
        compiler_params=pltpu.CompilerParams(
            collective_id=0, has_side_effects=True, vmem_limit_bytes=VMEM_LIMIT
        ),
        name="evoformer",
    )(msa, pair, w, wmix, tmat, amino, poly, wshift.T, wfac.T, live, shifts)
    return msa + delta, pair + proj


def solution(mesh):
    in_specs = (P("seq", "res", None), P("res", "seq", None)) + (P(),) * 9
    out_specs = (P("seq", "res", None), P("res", "seq", None))
    return jax.shard_map(
        on_device, mesh=mesh, in_specs=in_specs, out_specs=out_specs, check_vma=False
    )
```

```python
import math

import jax
import jax.numpy as jnp
from jax import lax
from jax.experimental import pallas as pl
from jax.experimental.pallas import tpu as pltpu
from jax.sharding import PartitionSpec as P

MESH = pl.DeviceIdType.MESH
F32 = jnp.float32
BF16 = jnp.bfloat16
LOG2E = math.log2(math.e)
VMEM_LIMIT = 58 * 1024 * 1024

N_RES, N_SEQ = 32, 4
S_LOC, I_LOC, J_LOC = 32, 24, 192
CM, CZ, HEADS, HD, OPM = 256, 128, 8, 32, 32
RES = 768
Q_CHUNK, K_CHUNK = 384, 256
OFFSETS = [((k * 11) % 32 // 8, (k * 11) % 8 // 4, (k * 11) % 4) for k in range(1, N_RES)]
YZ = [((k * 3) % 8 // 4, (k * 3) % 4) for k in range(8)]
J_BLOCKS = 2
JC = J_BLOCKS * I_LOC


def lane_iota(shape):
    return lax.broadcasted_iota(jnp.int32, shape, len(shape) - 1)


def in_slot(lane, k):
    return (lane >= k * 32) & (lane < (k + 1) * 32)


def layer_norm(x):
    centre = jnp.mean(x, axis=-1, keepdims=True)
    d = x - centre
    spread = jnp.mean(d * d, axis=-1, keepdims=True)
    return d * lax.rsqrt(spread + 1e-05)


def nt_dot(a, b, precision=None):
    return lax.dot_general(
        a, b, (((1,), (1,)), ((), ())), precision=precision, preferred_element_type=F32
    )


def exchange_lanes(tiles, width):
    lane = lane_iota(tiles[0].shape)
    tiles, bit = list(tiles), 1
    while bit < len(tiles):
        low = lax.rem(lane, 2 * bit * width) < bit * width
        new = list(tiles)
        for k in range(len(tiles)):
            if not k & bit:
                a, b = tiles[k], tiles[k | bit]
                new[k] = jnp.where(low, a, pltpu.roll(b, bit * width, 1))
                new[k | bit] = jnp.where(low, pltpu.roll(a, 128 - bit * width, 1), b)
        tiles, bit = new, 2 * bit
    return tiles


def remote(src, dst, a, b, d, q):
    return pltpu.make_async_remote_copy(
        src_ref=src, dst_ref=dst, send_sem=a, recv_sem=b, device_id=(d, q), device_id_type=MESH
    )


def kernel(
    msa_hbm, pair_hbm, w_hbm, wmix_hbm, tmat_hbm, amino, poly, wshift_t, wfac_t, live, shifts,
    delta_hbm, proj_hbm,
    msa, pair, w, wmix, tmat, dbuf, pbuf,
    btmp, bsend, b1, b2, br, bias, pgate, gate, qsend, recv, qs, ks, vs, acc, ret, back,
    wrep, wfac, fac, tr, lbuf, xbuf, lall, rall, lw, tcat, lhs, amat,
    ss, rs, s1, r1, s2, r2, s3, r3, sb, rb, sl, rl, sx, rx, sr, rr_sem, loc, ins, outs,
):
    r, s = lax.axis_index("res"), lax.axis_index("seq")
    h, z = lax.div(r, 4), lax.rem(r, 4)
    y_lo, b = lax.rem(h, 2), lax.div(r, 8)
    s_c = s + 1 - 2 * lax.rem(s, 2)
    xs = [lax.rem(b + k, 4) * 8 for k in range(4)]
    ys = [lax.rem(y_lo + k, 2) * 4 for k in range(2)]
    zs = [lax.rem(z + k, 4) for k in range(4)]
    seqs = [lax.rem(s + k, 4) for k in range(4)]
    partners = [xs[i] + ys[j] + zs[k] for i, j, k in OFFSETS]

    loads = [
        pltpu.make_async_copy(src, dst, ins.at[6 + n])
        for n, (src, dst) in enumerate(
            ((msa_hbm, msa), (w_hbm, w), (wmix_hbm, wmix), (tmat_hbm, tmat))
        )
    ]
    pair_loads = [
        pltpu.make_async_copy(pair_hbm.at[pl.ds(4 * n, 4)], pair.at[pl.ds(4 * n, 4)], ins.at[n])
        for n in range(6)
    ]
    for cp in loads[:2] + pair_loads + loads[2:]:
        cp.start()

    barrier = pltpu.get_barrier_semaphore()

    def greet(d, q):
        pl.semaphore_signal(barrier, inc=1, device_id=(d, q), device_id_type=MESH)

    for d in partners:
        greet(d, s)
    for k in range(4):
        greet(h * 4 + k, seqs[2])
    for k in range(1, N_SEQ):
        greet(r, seqs[k])
    for dy, dz in YZ:
        for k in range(N_SEQ):
            if dy or dz or k:
                greet(8 * b + ys[dy] + zs[dz], seqs[k])

    loads[0].wait()
    loads[1].wait()
    normed = layer_norm(msa[...].reshape(S_LOC * I_LOC, CM)).astype(BF16)
    lane3 = lane_iota((8, I_LOC, 128))
    for part in range(3):
        out = jnp.dot(normed, w[:, part * CM : (part + 1) * CM], preferred_element_type=F32)
        if part == 0:
            out = out * F32(LOG2E / math.sqrt(HD))
        for t in range(2):
            cols = out[:, t * 128 : (t + 1) * 128].reshape(8, 4, I_LOC, 128)
            for a in range(4):
                tile = None
                for k in range(4):
                    piece = cols[:, k]
                    if (k - a) % 4:
                        piece = pltpu.roll(piece, (k - a) % 4 * 32, 2)
                    tile = piece if tile is None else jnp.where(in_slot(lane3, k), piece, tile)
                tile = tile.astype(BF16)
                for g in range(4):
                    for half in range(2):
                        qsend[(t * 4 + a) * 4 + g, half, part] = tile[g * 2 + half]

    btmp[...] = jnp.zeros_like(btmp)
    chunk = 4
    for cp in pair_loads:
        cp.wait()
    for i0 in range(0, I_LOC, chunk):
        zn = layer_norm(pair[i0 : i0 + chunk].reshape(chunk * J_LOC, CZ))
        bb = nt_dot(wshift_t[...], zn, lax.Precision.HIGHEST)
        for i in range(chunk):
            rows, col = slice((i0 + i) * HEADS, (i0 + i + 1) * HEADS), i * J_LOC
            btmp[0, rows, :] = bb[:, col : col + 128]
            btmp[1, rows, 0:64] = bb[:, col + 128 : col + J_LOC]
    odd = jnp.full((I_LOC, 128), lax.rem(s, 2), jnp.int32) > 0
    swap = jnp.full((I_LOC, 128), lax.rem(h, 2), jnp.int32) > 0
    lane24 = lane_iota((I_LOC, 128))
    low24 = lane24 < 64
    for hh in range(HEADS):
        v0, v1 = (btmp[n, pl.ds(hh, I_LOC, stride=HEADS), :] for n in range(2))
        t0, t1 = pltpu.roll(v0, 64, 1), pltpu.roll(v1, 64, 1)
        bsend[hh, 0] = jnp.where(odd, jnp.where(low24, t0, t1), v0).astype(BF16)
        part = jnp.where(odd, v0, v1)
        bsend[hh, 1] = jnp.where(swap, pltpu.roll(part, 64, 1), part).astype(BF16)

    pl.semaphore_wait(barrier, 31 + 4 + 3 + 31)

    def send_rows(half, some):
        for d in some:
            remote(qsend.at[d, half], recv.at[half, r], ss, rs.at[half], d, s).start()

    for half in range(2):
        pltpu.make_async_copy(qsend.at[r, half], recv.at[half, r], rs.at[half]).start()

    pltpu.make_async_copy(bsend.at[h], b1.at[h], r1).start()
    for i in range(4):
        for j in range(2):
            if i or j:
                d = xs[i] + ys[j] + z
                remote(bsend.at[lax.div(d, 4)], b1.at[h], s1, r1, d, s).start()

    send_rows(0, partners[:16])

    pgate[...] = jnp.dot(normed, w[:, 3 * CM :], preferred_element_type=F32).astype(BF16).astype(F32)
    for t in range(2):
        cols = jax.nn.sigmoid(pgate[:, t * 128 : (t + 1) * 128]).reshape(8, 4, I_LOC, 128)
        for a in range(4):
            tile = None
            for k in range(4):
                piece = cols[:, k]
                if (k - a) % 4:
                    piece = pltpu.roll(piece, (k - a) % 4 * 32, 2)
                tile = piece if tile is None else jnp.where(in_slot(lane3, k), piece, tile)
            for g in range(4):
                for half in range(2):
                    gate[half, t * 4 + a, g] = tile[g * 2 + half]

    pltpu.make_async_copy(bsend, b1, r1).wait()
    for k in range(HEADS):
        b2[k] = b1[k, 0]
    for k in range(4):
        b2[8 + k] = jnp.where(
            low24, b1[2 * k, 1].astype(F32), b1[2 * k + 1, 1].astype(F32)
        ).astype(BF16)
    slot = s * 4 + z
    mine2 = lax.div(s, 2) * 4 + z
    own2 = pltpu.make_async_copy(b2, br.at[slot], loc.at[0])
    own2.start()
    for k in range(1, 8):
        zz, q = zs[k // 2], seqs[k % 2 * 2]
        remote(b2, br.at[slot], s2, r2.at[mine2], h * 4 + zz, q).start()
    remote(b2, br.at[slot], s3, r3.at[z], r, s_c).start()
    send_rows(0, partners[16:])

    loads[2].wait()
    loads[3].wait()
    for hh in range(HEADS):
        for k in range(4):
            wrep[hh * 128 + k * 32 : hh * 128 + (k + 1) * 32, :] = wmix[hh * HD : (hh + 1) * HD, :]
    wfac[...] = jnp.concatenate([wfac_t[...], jnp.zeros((64, CM), BF16)], axis=0)
    for e in range(OPM):
        t = tmat[pl.ds(e, OPM, stride=OPM), :]
        head = t.astype(BF16)
        tcat[e * 32 : (e + 1) * 32, 0:128] = head
        tcat[e * 32 : (e + 1) * 32, 128:256] = (t - head.astype(F32)).astype(BF16)
    acc[...] = jnp.zeros_like(acc)
    amino_row = amino[...].reshape(1, RES)
    poly_row = poly[...].reshape(1, RES)

    def column(row, n):
        tile = row[:, n * 128 : (n + 1) * 128].astype(F32)
        return jnp.transpose(jnp.broadcast_to(tile, (128, 128)), (1, 0))

    amino_col = [column(amino_row, n) for n in range(6)]
    for n in range(6):
        fac[n * 128 : (n + 1) * 128, :] = column(poly_row, n)

    remote(br.at[pl.ds(0, 7)], br.at[pl.ds(0, 7)], s2, r1, r, s_c).wait_send()
    send_rows(1, partners)

    shift = shifts[h]
    poly_f = poly_row.astype(F32)

    def build(zz, pair_n):
        for parity in range(2):
            hh = 2 * pair_n + parity
            row = pl.multiple_of((hh * 4 + zz) * I_LOC, 8)
            own = fac[pl.ds(row, I_LOC), :]
            full = [br[q * 4 + zz, hh].astype(F32) for q in range(4)]
            part = [br[q * 4 + zz, 8 + pair_n].astype(F32) for q in range(4)]
            for q in range(4):
                if q % 2 != parity:
                    part[q] = pltpu.roll(part[q], 64, 1)
            tiles = [
                full[0], jnp.where(low24, part[0], part[1]), full[1],
                full[2], jnp.where(low24, part[2], part[3]), full[3],
            ]
            for n in range(6):
                cols = slice(n * 128, (n + 1) * 128)
                val = tiles[n] + jnp.where(own != poly_f[:, cols], shift, F32(0.0))
                val = jnp.where(amino_row[:, cols] > 0, val * F32(LOG2E), F32(-1e9))
                bias[pl.ds(row, I_LOC), cols] = val

    def finish_z(zz):
        remote(br.at[pl.ds(0, 2)], br.at[pl.ds(0, 2)], s3, r3.at[zz], r, s_c).wait_recv()

        def step(pair_n, c):
            build(zz, pair_n)
            return c

        lax.fori_loop(0, 4, step, 0)

    own2.wait()
    before = None
    for k in (0, 3, 2, 1):
        for y in range(2):
            if k or y:
                zz, q = zs[k], seqs[2 * y]
                at = q * 4 + zz
                remote(
                    b2, br.at[at], s2, r2.at[lax.div(q, 2) * 4 + zz], h * 4 + zz, q
                ).wait_recv()
                remote(br.at[at], br.at[at], s3, r3.at[zz], r, s_c).start()
        if before is not None:
            finish_z(before)
        before = zs[k]
    finish_z(before)

    lane_q = lane_iota((Q_CHUNK, 128))
    lane = lane_iota((RES, 128))
    for half in range(2):
        pltpu.make_async_copy(recv.at[half], recv.at[half], rs.at[half]).wait()
        qs[...] = recv[half, :, 0].astype(F32).reshape(RES, 128).astype(BF16)
        kf = recv[half, :, 1].astype(F32).reshape(RES, 128)
        for n in range(6):
            rows = slice(n * 128, (n + 1) * 128)
            ks[rows, :] = jnp.where(amino_col[n] > 0, kf[rows], F32(0.0)).astype(BF16)
        vs[...] = recv[half, :, 2].astype(F32).reshape(RES, 128).astype(BF16)

        def one_row(rr):
            slot = in_slot(lane, rr)
            xv = jnp.where(slot, vs[...].astype(F32), F32(1.0)).astype(BF16)
            xk = ks[...]
            slot_q = in_slot(lane_q, rr)
            for q0 in range(0, RES, Q_CHUNK):
                rows = slice(q0, q0 + Q_CHUNK)
                xq = jnp.where(slot_q, qs[rows, :].astype(F32), F32(0.0)).astype(BF16)
                o = m = None
                for k0 in range(0, RES, K_CHUNK):
                    keys = slice(k0, k0 + K_CHUNK)
                    sc = nt_dot(xq, xk[keys]) + bias[rows, keys]
                    m1 = jnp.max(sc, axis=-1, keepdims=True)
                    p = jnp.exp2(sc - m1).astype(BF16)
                    o1 = jnp.dot(p, xv[keys], preferred_element_type=F32)
                    if o is None:
                        o, m = o1, m1
                    else:
                        top = jnp.maximum(m, m1)
                        o = o * jnp.exp2(m - top) + o1 * jnp.exp2(m1 - top)
                        m = top
                o = o / pltpu.roll(o, 32, 1)
                acc[half, rows, :] = jnp.where(slot_q, o, acc[half, rows, :])

        def two_rows(rr, c):
            one_row(2 * rr)
            one_row(2 * rr + 1)
            return c

        lax.fori_loop(0, 2, two_rows, 0)
        ret[half] = acc[half].reshape(N_RES, I_LOC, 128).astype(BF16)
        pltpu.make_async_copy(ret.at[half, r], back.at[half, r], rb.at[half]).start()

        for d in partners:
            remote(ret.at[half, d], back.at[half, r], sb.at[half], rb.at[half], d, s).start()

    def send_left(half):
        pltpu.make_async_copy(lbuf.at[half], lall.at[s, half], rl).start()
        for k in range(1, N_SEQ):
            remote(lbuf.at[half], lall.at[s, half], sl, rl, r, seqs[k]).start()

    blk_r = lax.rem(r, 8)

    def send_x(half):
        block = xbuf.at[half, b]
        for k in range(1, 4):
            remote(block, block, sx.at[half], rx.at[half], xs[k] + ys[0] + zs[0], s).start()

    def wait_x(half):
        three = xbuf.at[half, pl.ds(0, 3)]
        remote(three, three, sx.at[half], rx.at[half], r, s_c).wait_recv()

    def send_right(half, k, group):
        dy, dz = YZ[k // 4]
        x = seqs[k % 4]
        src, dst, sem = xbuf.at[half, x], rall.at[blk_r, s, half], rr_sem.at[blk_r]
        if k:
            remote(src, dst, sr.at[group], sem, 8 * b + ys[dy] + zs[dz], x).start()
        else:
            pltpu.make_async_copy(src, dst, sem).start()

    lane16 = lane_iota((16, 128))
    lane96 = lane_iota((4 * I_LOC, 128))
    for n in range(6):
        tr[n * 128 : (n + 1) * 128, :] = amino_col[n]
    own_live = tr[pl.ds(pl.multiple_of(r * I_LOC, 8), I_LOC), :]
    for half in range(2):
        pltpu.make_async_copy(back.at[half], back.at[half], rb.at[half]).wait()
        heads = [
            (back[half, 4 * hh : 4 * hh + 4].astype(F32) * gate[half, hh]).reshape(4 * I_LOC, 128)
            for hh in range(HEADS)
        ]
        gated = jnp.concatenate(
            [
                jnp.concatenate(
                    [jnp.where(in_slot(lane96, k), t, F32(0.0)).astype(BF16) for t in heads], axis=1
                )
                for k in range(4)
            ],
            axis=0,
        )
        delta = jnp.dot(gated, wrep[...], preferred_element_type=F32).reshape(16, I_LOC, CM)
        fams = []
        for k in range(4):
            for g in range(4):
                row = g * 8 + half * 4 + k
                step = live[s * S_LOC + row].astype(F32) * delta[k * 4 + g]
                dbuf[row] = step
                fams.append(msa[row] + step)
        y = layer_norm(jnp.concatenate(fams, axis=0)).astype(BF16)
        f = nt_dot(y, wfac[...])
        for k in range(4):
            for g in range(4):
                on = live[s * S_LOC + g * 8 + half * 4 + k].astype(F32)
                at = (k * 4 + g) * I_LOC
                fac[at : at + I_LOC, :] = f[at : at + I_LOC] * (on * own_live)
        for i0 in range(0, I_LOC, 4):
            tile = None
            for k in range(4):
                i = i0 + k
                f = fac[pl.ds(i, 16, stride=I_LOC), :]
                moved = pltpu.roll(f, k * 32, 1) if k else f
                tile = moved if tile is None else jnp.where(in_slot(lane16, k), moved, tile)
                ft = jnp.transpose(f, (1, 0))[OPM : 2 * OPM, :]
                tr[i * OPM : (i + 1) * OPM, :] = jnp.concatenate(
                    [ft, jnp.zeros((OPM, 112), F32)], axis=1
                )
            lbuf[half, :, i0 * 32 : (i0 + 4) * 32] = tile.astype(BF16)
        send_left(half)
        for e0 in range(0, OPM, 8):
            tile = tr[pl.ds(e0, I_LOC, stride=OPM), :]
            for k in range(1, 8):
                moved = pltpu.roll(tr[pl.ds(e0 + k, I_LOC, stride=OPM), :], k * 16, 1)
                tile = jnp.where(lane24 >= k * 16, moved, tile)
            xbuf[half, b, :, e0 * 16 : (e0 + 8) * 16] = tile.astype(BF16)
        send_x(half)
        wait_x(half)
        if half == 0:
            for k in range(16):
                send_right(0, k, 4)
        else:
            for k in range(8):
                send_right(1, k, 0)
            out_delta = pltpu.make_async_copy(dbuf, delta_hbm, outs.at[16])
            out_delta.start()

    def take_left():
        pltpu.make_async_copy(lall, lall, rl).wait()
        left = lall[...].reshape(N_SEQ * S_LOC, I_LOC * OPM)
        for n in range(6):
            lw[n] = left[:, n * 128 : (n + 1) * 128]

    def wait_sent(group, blocks):
        for size, ref in ((8, rall.at[0]), (2, rall.at[0, 0]), (1, rall.at[0, 0, 0])):
            for _ in range(blocks // size):
                remote(ref, ref, sr.at[group], r1, r, s_c).wait_send()
            blocks %= size

    def send_group(group):
        for k in range(8 * group, 8 * group + 8):
            send_right(0, k, group)
            send_right(1, k, group)

    count = lax.fori_loop(0, 128, lambda k, c: c + live[k], jnp.int32(0)).astype(F32)
    inv = 1.0 / jnp.maximum(jnp.full((1, 128), count, F32), 1.0)

    wait_sent(0, 7)
    for k in range(8, 16):
        send_right(1, k, 1)
    send_group(2)

    def blocks_of(c):
        blocks = []
        for t in range(J_BLOCKS):
            kk = lax.rem((c * J_BLOCKS + t) * 3, 8)
            blocks.append(
                lax.rem(y_lo + 2 - lax.div(kk, 4), 2) * 4 + lax.rem(z + 4 - lax.rem(kk, 4), 4)
            )
        return blocks

    def result(c, t, p, blk):
        some = pl.ds(12 * p, 12)
        return pltpu.make_async_copy(
            pbuf.at[blk, some],
            proj_hbm.at[some, pl.ds(pl.multiple_of(blk * I_LOC, 8), I_LOC)],
            outs.at[c * 4 + t * 2 + p],
        )

    def one_chunk(c, carry):
        blocks = blocks_of(c)
        for blk in blocks:
            pltpu.make_async_copy(rall.at[blk], rall.at[blk], rr_sem.at[blk]).wait()
        for ge in range(4):
            cols = slice(ge * 128, (ge + 1) * 128)
            tiles = [
                jnp.concatenate([rall[blk, q, half, :, cols].astype(F32) for blk in blocks], axis=0)
                for q in range(N_SEQ)
                for half in range(2)
            ]
            for e, tile in enumerate(exchange_lanes(tiles, 16)):
                lhs[(ge * 8 + e) * JC : (ge * 8 + e + 1) * JC, :] = tile.astype(BF16)

        @pl.when(c == 0)
        def _():
            wait_sent(1, 8)
            send_group(3)
            take_left()

        def spread(p, cc):
            w2 = jnp.concatenate([lw[2 * p], lw[2 * p + 1]], axis=1)
            o = jnp.dot(lhs[...], w2, preferred_element_type=F32).astype(BF16)
            for t in range(2):
                for g in range(8):
                    tiles = [
                        o[(4 * g + k) * JC : (4 * g + k + 1) * JC, t * 128 : (t + 1) * 128]
                        for k in range(4)
                    ]
                    for m, tile in enumerate(exchange_lanes(tiles, 32)):
                        amat[(2 * p + t) * 4 + m, :, g * 128 : (g + 1) * 128] = tile
            return cc

        lax.fori_loop(0, 3, spread, 0)

        def finish(p, cc):
            some = pl.ds(12 * p, 12)
            o = jnp.dot(amat[some].reshape(12 * JC, 1024), tcat[...], preferred_element_type=F32)
            o = ((o[:, :128] + o[:, 128:]) * inv).reshape(12, JC, CZ)
            for t, blk in enumerate(blocks):
                pbuf[blk, some] = o[:, t * I_LOC : (t + 1) * I_LOC]
                result(c, t, p, blk).start()
            return cc

        lax.fori_loop(0, 2, finish, 0)
        return carry

    lax.fori_loop(0, 8 // J_BLOCKS, one_chunk, 0)

    out_delta.wait()

    def result_out(c, carry):
        for t, blk in enumerate(blocks_of(c)):
            for p in range(2):
                result(c, t, p, blk).wait()
        return carry

    lax.fori_loop(0, 8 // J_BLOCKS, result_out, 0)
    remote(bsend.at[pl.ds(0, 7)], b1.at[pl.ds(0, 7)], s1, r1, r, s_c).wait_send()
    remote(br.at[pl.ds(0, 8)], br.at[pl.ds(0, 8)], s3, r1, r, s_c).wait_send()
    remote(qsend.at[pl.ds(0, 31)], qsend.at[pl.ds(0, 31)], ss, r1, r, s_c).wait_send()
    for half in range(2):
        remote(
            ret.at[half, pl.ds(0, 31)], ret.at[half, pl.ds(0, 31)], sb.at[half], r1, r, s_c
        ).wait_send()
    remote(lall.at[pl.ds(0, 3)], lall.at[pl.ds(0, 3)], sl, r1, r, s_c).wait_send()
    wait_sent(2, 16)
    wait_sent(3, 16)
    wait_sent(4, 15)
    for half in range(2):
        three = xbuf.at[half, pl.ds(0, 3)]
        remote(three, three, sx.at[half], r1, r, s_c).wait_send()


def on_device(msa, pair, amino, poly, live, w, wshift, shifts, wmix, wfac, tmat):
    dma = pltpu.SemaphoreType.DMA
    vm = pl.BlockSpec(memory_space=pltpu.VMEM)
    sm = pl.BlockSpec(memory_space=pltpu.SMEM)
    hbm = pl.BlockSpec(memory_space=pl.ANY)
    delta, proj = pl.pallas_call(
        kernel,
        out_shape=(
            jax.ShapeDtypeStruct((S_LOC, I_LOC, CM), F32),
            jax.ShapeDtypeStruct((I_LOC, J_LOC, CZ), F32),
        ),
        in_specs=[hbm] * 5 + [vm] * 4 + [sm] * 2,
        out_specs=(hbm, hbm),
        scratch_shapes=[
            pltpu.VMEM((S_LOC, I_LOC, CM), F32),
            pltpu.VMEM((I_LOC, J_LOC, CZ), F32),
            pltpu.VMEM((CM, 4 * CM), BF16),
            pltpu.VMEM((CM, CM), BF16),
            pltpu.VMEM((OPM * OPM, CZ), F32),
            pltpu.VMEM((S_LOC, I_LOC, CM), F32),
            pltpu.VMEM((8, I_LOC, I_LOC, CZ), F32),
            pltpu.VMEM((2, I_LOC * HEADS, 128), F32),
            pltpu.VMEM((HEADS, 2, I_LOC, 128), BF16),
            pltpu.VMEM((HEADS, 2, I_LOC, 128), BF16),
            pltpu.VMEM((12, I_LOC, 128), BF16),
            pltpu.VMEM((N_SEQ * 4, 12, I_LOC, 128), BF16),
            pltpu.VMEM((RES, RES), F32),
            pltpu.VMEM((RES, CM), F32),
            pltpu.VMEM((2, HEADS, 4, I_LOC, 128), F32),
            pltpu.VMEM((N_RES, 2, 3, I_LOC, 128), BF16),
            pltpu.VMEM((2, N_RES, 3, I_LOC, 128), BF16),
            pltpu.VMEM((RES, 128), BF16),
            pltpu.VMEM((RES, 128), BF16),
            pltpu.VMEM((RES, 128), BF16),
            pltpu.VMEM((2, RES, 128), F32),
            pltpu.VMEM((2, N_RES, I_LOC, 128), BF16),
            pltpu.VMEM((2, N_RES, I_LOC, 128), BF16),
            pltpu.VMEM((1024, CM), BF16),
            pltpu.VMEM((128, CM), BF16),
            pltpu.VMEM((RES, 128), F32),
            pltpu.VMEM((I_LOC * OPM, 128), F32),
            pltpu.VMEM((2, 16, I_LOC * OPM), BF16),
            pltpu.VMEM((2, 4, I_LOC, OPM * 16), BF16),
            pltpu.VMEM((N_SEQ, 2, 16, I_LOC * OPM), BF16),
            pltpu.VMEM((8, N_SEQ, 2, I_LOC, OPM * 16), BF16),
            pltpu.VMEM((6, N_SEQ * S_LOC, 128), BF16),
            pltpu.VMEM((1024, 256), BF16),
            pltpu.VMEM((OPM * JC, 128), BF16),
            pltpu.VMEM((I_LOC, JC, 1024), BF16),
            dma, dma((2,)), dma, dma, dma, dma((8,)), dma, dma((4,)),
            dma((2,)), dma((2,)), dma, dma, dma((2,)), dma((2,)),
            dma((5,)), dma((8,)), dma((1,)),
            dma((10,)), dma((17,)),
        ],
        compiler_params=pltpu.CompilerParams(
            collective_id=0, has_side_effects=True, vmem_limit_bytes=VMEM_LIMIT
        ),
        name="evoformer",
    )(msa, pair, w, wmix, tmat, amino, poly, wshift.T, wfac.T, live, shifts)
    return msa + delta, pair + proj


def solution(mesh):
    in_specs = (P("seq", "res", None), P("res", "seq", None)) + (P(),) * 9
    out_specs = (P("seq", "res", None), P("res", "seq", None))
    return jax.shard_map(
        on_device, mesh=mesh, in_specs=in_specs, out_specs=out_specs, check_vma=False
    )
```
